128 devices in a mesh: cfg: 2 (over core), seq: 32 (over y, z_lo, x), head: 2 (over z_hi).
Axes of the slice: x: 4, y: 4, z: 4 (z_hi: 2, z_lo: 2; z = z_hi * 2 + z_lo), core: 2. Of those that a mesh axis runs over, the one named last changes fastest.
Arguments:
- hidden: bfloat16 [2, 7168, 5120], P('cfg', 'seq', 'head'), may hold values from -6 to 6
- queries: bfloat16 [2, 7168, 2560], P('cfg', 'seq', 'head'), may hold values from -66 to 66
- keys: bfloat16 [2, 7168, 2560], P('cfg', 'seq', 'head'), may hold values from -12 to 12
- values: bfloat16 [2, 7168, 2560], P('cfg', 'seq', 'head'), may hold values from -6 to 6
- output_weight: bfloat16 [2560, 5120], P('head'), may hold values from -0.125 to 0.125
- adapter_down_weight: bfloat16 [8, 2560, 32], P(None, 'head'), may hold values from -0.125 to 0.125
- adapter_up_weight: bfloat16 [8, 32, 5120], P(None, None, 'head'), may hold values from -1 to 1
- request_adapters: int32 [4], replicated, may hold values from 0 to 7
- request_length: int32 [4], replicated, may hold values from 1 to 4480, 7168 in all
Outputs:
- guided: bfloat16 [7168, 5120], P('seq', 'head')
The draws below stay inside these ranges and needn't reach their ends.
All inputs are finite; a program needn't handle non-finite values.
Results may differ from the reference program's by a relative error of at most 0.028.
Values may be sent and summed in bfloat16 or wider, within the bound.
A program may use at most 192 MiB of HBM per device.

```python
import math
import jax
import jax.numpy as jnp
import numpy as np
from jax import lax

MODEL_WIDTH = 5120
HEADS = 20
HS = 128
ADAPTER_RANK = 32
ADAPTER_TOTAL = 8
REQS = 4
BRANCH_TOKENS = 7168
HEAD_FEATURES = 2560
LONGEST = 4480


def shared_base(key):
    return jnp.clip(jax.random.normal(key, (2, BRANCH_TOKENS, HEAD_FEATURES), jnp.float32), -6.0, 6.0)


def draw_keys(key, part):
    base = shared_base(key)
    return (2.0 * base).astype(jnp.bfloat16)


def draw_queries(key, part):
    key = jax.random.fold_in(key, 1)
    result = 2.0 * jnp.clip(jax.random.normal(key, (2, BRANCH_TOKENS, HEAD_FEATURES), jnp.float32), -6.0, 6.0)
    return result.astype(jnp.bfloat16)


def place_ends(array, stream_key, low, top_value):
    longest = array.shape.index(max(array.shape))
    spots = []
    for shift in (0, 1):
        where = [jax.random.randint(jax.random.fold_in(stream_key, axis), (), 0, length) for axis, length in enumerate(array.shape)]
        where[longest] = (where[longest] + shift) % array.shape[longest]
        spots.append(tuple(where))
    return array.at[spots[0]].set(low).at[spots[1]].set(top_value)


def levels(own_key, shape, pieces, least, top_value):
    gain = 1.0
    for dim, blocks in pieces:
        steps = jax.random.uniform(jax.random.fold_in(jax.random.fold_in(own_key, 6), dim), (blocks,), jnp.float32, least / len(pieces), top_value / len(pieces))
        gain = gain * jnp.repeat(jnp.exp(steps), shape[dim] // blocks).reshape((-1,) + (1,) * (len(shape) - 1 - dim))
    return gain


def profile(number_of, total, limit, lean):
    weights = [(1 << 20) // math.isqrt(rank ** lean) + 1 for rank in range(2, number_of + 1)]
    rest, given = total - limit - (number_of - 1), [1] * (number_of - 1)
    while rest > 0:
        movable = [i for i in range(number_of - 1) if given[i] < limit]
        whole, budget = sum([weights[i] for i in movable]), rest
        for i in movable:
            extra = min(limit - given[i], max(1, budget * weights[i] // whole), rest)
            given[i] = given[i] + extra
            rest = rest - extra
    return np.array([limit] + given)


def ragged_sizes(own_key, number_of, total, most, slope):
    if number_of == 2:
        one = jax.random.randint(own_key, (), max(1, total - most), min(most, total - 1) + 1)
        return jnp.stack([one, total - one])
    sizes = jnp.asarray(profile(number_of, total, most, slope), jnp.int32)
    pairs = (number_of - 1) // 2
    giver, sink = sizes[1:1 + 2 * pairs:2], sizes[2:2 + 2 * pairs:2]
    margin = jnp.minimum(giver - 1, most - sink)
    moved = jax.random.randint(jax.random.fold_in(own_key, 1), (pairs,), 0, 1 << 20) % (margin + 1)
    sizes = sizes.at[1:1 + 2 * pairs:2].set(giver - moved).at[2:2 + 2 * pairs:2].set(sink + moved)
    return sizes[jax.random.permutation(jax.random.fold_in(own_key, 2), number_of)]


def centred(rng, extent, scale, bound, pieces=(), kind=jnp.bfloat16):
    drawn = jax.random.normal(rng, extent, jnp.float32) * scale
    if len(pieces) > 0:
        drawn = levels(rng, extent, pieces, -0.22, 0.18) * drawn
    return jnp.clip(drawn, min=-bound, max=bound).astype(kind)


def setup_inputs(seed: int = 0) -> dict:
    arg_keys = jax.random.split(jax.random.key(seed), 10)
    return {
        "hidden": centred(arg_keys[0], (2, BRANCH_TOKENS, MODEL_WIDTH), 1.0, 6.0, ((0, 2), (1, 32), (2, 2))),
        "queries": draw_queries(jax.random.fold_in(arg_keys[9], 71), 0),
        "keys": draw_keys(jax.random.fold_in(arg_keys[9], 71), 0),
        "values": centred(arg_keys[3], (2, BRANCH_TOKENS, HEAD_FEATURES), 1.0, 6.0, ((0, 2), (1, 32), (2, 2))),
        "output_weight": centred(arg_keys[4], (HEAD_FEATURES, MODEL_WIDTH), HEAD_FEATURES ** -0.5, 0.125, ((0, 2),)),
        "adapter_down_weight": centred(arg_keys[5], (ADAPTER_TOTAL, HEAD_FEATURES, ADAPTER_RANK), HEAD_FEATURES ** -0.5, 0.125, ((1, 2),)),
        "adapter_up_weight": centred(arg_keys[6], (ADAPTER_TOTAL, ADAPTER_RANK, MODEL_WIDTH), ADAPTER_RANK ** -0.5, 1.0, ((2, 2),)),
        "request_adapters": place_ends(jax.random.randint(arg_keys[7], (REQS,), 0, ADAPTER_TOTAL), jax.random.fold_in(arg_keys[7], 1), 0, ADAPTER_TOTAL - 1).astype(jnp.int32),
        "request_length": ragged_sizes(arg_keys[8], REQS, BRANCH_TOKENS, LONGEST, 0).astype(jnp.int32),
    }


guide_scale = 5.0

def reference(hidden, queries, keys, values, output_weight, adapter_down_weight, adapter_up_weight, request_adapters, request_length):
    positions = jnp.arange(BRANCH_TOKENS, dtype=jnp.int32)
    request_ends = jnp.cumsum(request_length).astype(jnp.int32)
    request = lax.optimization_barrier(jnp.sum((positions[:, None] >= request_ends[None, :]).astype(jnp.int32), 1))
    adapter_slot = request_adapters[request]
    same_request = request[:, None] == request[None, :]
    inverse_root = 1.0 / math.sqrt(HS)

    def attend_head(triple):
        head_query, head_key, head_value = triple
        scores = jnp.dot(head_query, head_key.T, preferred_element_type=jnp.float32) * inverse_root
        scores = jnp.where(same_request, scores, -1e+30)
        row_max = lax.optimization_barrier(jnp.max(scores, 1, keepdims=True))
        expon = jnp.where(same_request, jnp.exp(scores - row_max), 0.0)
        row_total = lax.optimization_barrier(jnp.sum(expon, 1, keepdims=True))
        return jnp.dot(expon.astype(jnp.bfloat16), head_value, preferred_element_type=jnp.float32) / row_total
    output_rows = []
    for guidance_branch in range(2):
        split_query = queries[guidance_branch].reshape(BRANCH_TOKENS, HEADS, HS).transpose(1, 0, 2)
        split_key = keys[guidance_branch].reshape(BRANCH_TOKENS, HEADS, HS).transpose(1, 0, 2)
        split_value = values[guidance_branch].reshape(BRANCH_TOKENS, HEADS, HS).transpose(1, 0, 2)
        per_head = lax.map(attend_head, (split_query, split_key, split_value))
        attention_result = per_head.transpose(1, 0, 2).reshape(BRANCH_TOKENS, HEAD_FEATURES).astype(jnp.bfloat16)
        inner_sum = jnp.zeros((BRANCH_TOKENS, ADAPTER_RANK), jnp.float32)
        for adapter_index in range(ADAPTER_TOTAL):
            down_product = jnp.dot(attention_result, adapter_down_weight[adapter_index], preferred_element_type=jnp.float32)
            inner_sum = inner_sum + jnp.where(adapter_slot[:, None] == adapter_index, down_product, 0.0)
        inner_value = inner_sum.astype(jnp.bfloat16)
        adapter_term = jnp.zeros((BRANCH_TOKENS, MODEL_WIDTH), jnp.float32)
        for adapter_index in range(ADAPTER_TOTAL):
            up_product = jnp.dot(inner_value, adapter_up_weight[adapter_index], preferred_element_type=jnp.float32)
            adapter_term = adapter_term + jnp.where(adapter_slot[:, None] == adapter_index, up_product, 0.0)
        projected_output = jnp.dot(attention_result, output_weight, preferred_element_type=jnp.float32)
        output_rows.append(hidden[guidance_branch].astype(jnp.float32) + projected_output + adapter_term)
    guided = guide_scale * output_rows[0] + (1.0 - guide_scale) * output_rows[1]
    return guided.astype(jnp.bfloat16)
```

```python
import functools
import math

import jax
import jax.numpy as jnp
from jax import lax
from jax.experimental import pallas as pl
from jax.experimental.pallas import tpu as pltpu
from jax.sharding import PartitionSpec as P

MESH = pl.DeviceIdType.MESH
HS = 128
GUIDE = 5.0
BK = 512
ANY = pl.BlockSpec(memory_space=pl.ANY)
SMEM = pl.BlockSpec(memory_space=pltpu.SMEM)


def place(head, branch):
    p = (head // 2) * 3 + head % 2
    return (p // 4) * 8 + branch * 4 + p % 4


def role(s):
    p = (s // 8) * 4 + s % 4
    active = jnp.logical_and(p % 3 < 2, p < 15)
    head = (p // 3) * 2 + p % 3
    return active, head, (s // 4) % 2


def scatter_kernel(
    q_ref, k_ref, v_ref, hid_ref, kbuf, vbuf, qbuf, hbuf,
    send_sem, kv_sem, q_sem, hid_sem, fwd_sem,
):
    b = lax.axis_index("cfg")
    s = lax.axis_index("seq")
    g = lax.axis_index("head")
    rows = q_ref.shape[1]
    heads = q_ref.shape[2] // HS
    half = hbuf.shape[1]
    groups = kv_sem.shape[0]
    per = kbuf.shape[0] // groups

    other = pltpu.make_async_remote_copy(
        src_ref=hid_ref.at[0, :, pl.ds(pl.multiple_of((1 - b) * half, half), half)],
        dst_ref=hbuf,
        send_sem=hid_sem.at[0],
        recv_sem=hid_sem.at[1],
        device_id=(1 - b, s, g),
        device_id_type=MESH,
    )

    row0 = pl.multiple_of(s * rows, 32)
    qrow0 = pl.multiple_of((s // 2) * rows, 32)
    kind = (
        (k_ref, lambda: kbuf.at[pl.ds(row0, rows), :], kv_sem.at[s // (32 // groups)], 0),
        (v_ref, lambda: vbuf.at[pl.ds(row0, rows), :], kv_sem.at[s // (32 // groups)], 1),
        (q_ref, lambda: qbuf.at[pl.ds(qrow0, rows), :], q_sem, s % 2),
    )

    def each(i, act):
        h = (i + s) % heads
        target = place(h, b)
        for n, (src, dst, sem, core) in enumerate(kind):
            piece = src.at[0, :, pl.ds(pl.multiple_of(h * HS, HS), HS)]
            mine = jnp.logical_and(target == s, core == b)
            act(n, piece, dst(), sem, core, target, mine, i)

    def start(n, piece, dst, sem, core, target, mine, i):
        @pl.when(mine)
        def _():
            pltpu.make_async_copy(piece, dst, sem).start()

        @pl.when(jnp.logical_not(mine))
        def _():
            pltpu.make_async_remote_copy(
                src_ref=piece, dst_ref=dst, send_sem=send_sem.at[i * 3 + n], recv_sem=sem,
                device_id=(core, target, g), device_id_type=MESH,
            ).start()

    def finish(n, piece, dst, sem, core, target, mine, i):
        @pl.when(jnp.logical_not(mine))
        def _():
            pltpu.make_async_remote_copy(
                src_ref=piece, dst_ref=dst, send_sem=send_sem.at[i * 3 + n], recv_sem=sem,
                device_id=(core, target, g), device_id_type=MESH,
            ).wait_send()

    @pl.loop(0, heads)
    def _(i):
        each(i, start)

    other.start()

    active, _, _ = role(s)

    def forward(buf, n):
        part = buf.at[pl.ds(n * per, per), :]
        return pltpu.make_async_remote_copy(
            src_ref=part, dst_ref=part, send_sem=fwd_sem.at[0, n], recv_sem=fwd_sem.at[1, n],
            device_id=(1 - b, s, g), device_id_type=MESH,
        )

    def landed(buf, sem):
        pltpu.make_async_copy(buf, buf, sem).wait()

    for core, (got, came) in enumerate(((kbuf, vbuf), (vbuf, kbuf))):

        @pl.when(jnp.logical_and(active, b == core))
        def _():
            for n in range(groups):
                landed(got.at[pl.ds(n * per, per), :], kv_sem.at[n])
                forward(got, n).start()
            for n in range(groups):
                forward(got, n).wait_send()
                forward(came, n).wait_recv()
            landed(qbuf, q_sem)

    @pl.loop(0, heads)
    def _(i):
        each(i, finish)

    other.wait()


def attention_kernel(len_ref, q_ref, k_ref, v_ref, o_ref, s_ref, m_ref, l_ref, acc_ref):
    c = lax.axis_index("cfg")
    s = lax.axis_index("seq")
    active, _, _ = role(s)
    rows = q_ref.shape[0]
    tokens = k_ref.shape[0]
    factor = math.log2(math.e) / math.sqrt(HS)
    first = (2 * pl.program_id(0) + c) * rows
    last = first + rows - 1
    e0 = len_ref[0]
    e1 = e0 + len_ref[1]
    e2 = e1 + len_ref[2]

    def segment(pos):
        return (
            (pos >= e0).astype(jnp.int32)
            + (pos >= e1).astype(jnp.int32)
            + (pos >= e2).astype(jnp.int32)
        )

    @pl.when(active)
    def _():
        seg_first = segment(first)
        seg_last = segment(last)
        starts = (0, e0, e1, e2)
        ends = (e0, e1, e2, tokens)
        lo = jnp.int32(0)
        hi = jnp.int32(tokens)
        for n in range(4):
            lo = jnp.where(seg_first == n, starts[n], lo)
            hi = jnp.where(seg_last == n, ends[n], hi)
        base = (lo // 32) * 32
        blocks = pl.cdiv(hi - base, BK)
        single = seg_first == seg_last
        seg_q = segment(first + lax.broadcasted_iota(jnp.int32, (rows, 1), 0))
        q = q_ref[...]
        m_ref[...] = jnp.full_like(m_ref, -1e30)

        def lanes(x, op):
            out = x[:, :HS]
            for n in range(1, BK // HS):
                out = op(out, x[:, n * HS : (n + 1) * HS])
            return out

        @pl.loop(0, blocks)
        def _(n):
            logical = base + n * BK
            at = pl.multiple_of(jnp.minimum(logical, tokens - BK), 32)
            score = lax.dot_general(
                q, k_ref[pl.ds(at, BK), :], (((1,), (1,)), ((), ())),
                preferred_element_type=jnp.float32,
            )
            whole = jnp.logical_and(
                single, jnp.logical_and(logical >= lo, logical + BK <= hi)
            )

            @pl.when(whole)
            def _():
                s_ref[n] = score
                m_ref[...] = jnp.maximum(m_ref[...], lanes(score, jnp.maximum))

            @pl.when(jnp.logical_not(whole))
            def _():
                pos = at + lax.broadcasted_iota(jnp.int32, (1, BK), 1)
                seg_k = jnp.where(pos >= logical, segment(pos), -1)
                masked = jnp.where(seg_q == seg_k, score, -jnp.inf)
                s_ref[n] = masked
                m_ref[...] = jnp.maximum(m_ref[...], lanes(masked, jnp.maximum))

        top = jnp.max(m_ref[...], axis=1, keepdims=True)
        l_ref[...] = jnp.zeros_like(l_ref)
        acc_ref[...] = jnp.zeros_like(acc_ref)

        @pl.loop(0, blocks)
        def _(n):
            at = pl.multiple_of(jnp.minimum(base + n * BK, tokens - BK), 32)
            weight = jnp.exp2((s_ref[n] - top) * factor)
            l_ref[...] += lanes(weight, jnp.add)
            acc_ref[...] += jnp.dot(
                weight.astype(jnp.bfloat16), v_ref[pl.ds(at, BK), :],
                preferred_element_type=jnp.float32,
            )

        total = jnp.sum(l_ref[...], axis=1, keepdims=True)
        o_ref[...] = (acc_ref[...] / total).astype(o_ref.dtype)


def project_kernel(
    len_ref, ad_ref, o_ref, hid_ref, hbuf, w_ref, down_ref, up_ref, out_ref,
    att, wo, wm, downv, upv, hm, ho, dv, pm, psend, precv, isend, irecv, outv,
    load_sem, o_send, o_sem, att_sem, p_sem, i_sem, out_sem,
):
    b = lax.axis_index("cfg")
    s = lax.axis_index("seq")
    g = lax.axis_index("head")
    active, head, branch = role(s)
    rows, half = outv.shape
    width = 2 * half
    blocks = o_ref.shape[0] // rows
    mine = pl.multiple_of(b * half, half)

    loads = [
        (down_ref, downv),
        (w_ref.at[:, pl.ds(pl.multiple_of((1 - g) * width + b * half, half), half)], wo),
        (w_ref.at[:, pl.ds(pl.multiple_of(g * width + b * half, half), half)], wm),
        (up_ref.at[:, pl.ds(mine, half)], upv),
        (hid_ref.at[0, :, pl.ds(mine, half)], hm),
        (hbuf, ho),
    ]
    loads = [pltpu.make_async_copy(a, z, load_sem.at[n]) for n, (a, z) in enumerate(loads)]

    def send_o(i, go):
        j = 2 * i + b
        piece = o_ref.at[pl.ds(pl.multiple_of(i * rows, 32), rows), :]
        dst = att.at[branch, :, pl.ds(pl.multiple_of(head * HS, HS), HS)]
        here = jnp.logical_and(j == s, branch == b)

        @pl.when(here)
        def _():
            if go:
                pltpu.make_async_copy(piece, dst, o_sem).start()

        @pl.when(jnp.logical_not(here))
        def _():
            copy = pltpu.make_async_remote_copy(
                src_ref=piece, dst_ref=dst, send_sem=o_send.at[i], recv_sem=o_sem,
                device_id=(branch, j, g), device_id_type=MESH,
            )
            if go:
                copy.start()
            else:
                copy.wait_send()

    @pl.when(active)
    def _():
        @pl.loop(0, blocks)
        def _(i):
            send_o((i + s // 2) % blocks, True)

    for copy in loads:
        copy.start()

    pltpu.make_async_copy(att.at[b], att.at[b], o_sem).wait()
    swap = pltpu.make_async_remote_copy(
        src_ref=att.at[b], dst_ref=att.at[b], send_sem=att_sem.at[0], recv_sem=att_sem.at[1],
        device_id=(1 - b, s, g), device_id_type=MESH,
    )
    swap.start()
    swap.wait()
    dv[...] = (
        GUIDE * att[0].astype(jnp.float32) + (1.0 - GUIDE) * att[1].astype(jnp.float32)
    ).astype(jnp.bfloat16)

    def partner(src, dst, sems):
        return pltpu.make_async_remote_copy(
            src_ref=src, dst_ref=dst, send_sem=sems.at[0], recv_sem=sems.at[1],
            device_id=(b, s, 1 - g), device_id_type=MESH,
        )

    loads[0].wait()
    pos = s * rows + lax.broadcasted_iota(jnp.int32, (rows, 1), 0)
    e0 = len_ref[0]
    e1 = e0 + len_ref[1]
    e2 = e1 + len_ref[2]
    adapter = jnp.where(
        pos < e1,
        jnp.where(pos < e0, ad_ref[0], ad_ref[1]),
        jnp.where(pos < e2, ad_ref[2], ad_ref[3]),
    )
    rank = downv.shape[1] // 8
    lane = lax.broadcasted_iota(jnp.int32, (rows, downv.shape[1]), 1)
    picked = (lane // rank) == adapter
    inner = jnp.dot(dv[...], downv[...], preferred_element_type=jnp.float32)
    isend[...] = jnp.where(picked, inner, 0.0).astype(jnp.bfloat16)
    inner_copy = partner(isend, irecv, i_sem)
    inner_copy.start()

    cols = 256
    loads[1].wait()
    for n in range(half // cols):
        sl = pl.ds(n * cols, cols)
        psend[n] = jnp.dot(dv[...], wo[:, sl], preferred_element_type=jnp.float32).astype(jnp.bfloat16)
        partner(psend.at[n], precv.at[n], p_sem.at[n]).start()
    loads[2].wait()
    for n in range(half // cols):
        sl = pl.ds(n * cols, cols)
        pm[:, sl] = jnp.dot(dv[...], wm[:, sl], preferred_element_type=jnp.float32)
    for copy in loads[3:]:
        copy.wait()
    scale_m = jnp.where(b == 0, GUIDE, 1.0 - GUIDE).astype(jnp.float32)
    scale_o = jnp.where(b == 0, 1.0 - GUIDE, GUIDE).astype(jnp.float32)
    inner_copy.wait()
    both = jnp.where(
        picked, inner + irecv[...].astype(jnp.float32), 0.0
    ).astype(jnp.bfloat16)
    for n in range(half // cols):
        sl = pl.ds(n * cols, cols)
        pm[:, sl] += (
            jnp.dot(both, upv[:, sl], preferred_element_type=jnp.float32)
            + scale_m * hm[:, sl].astype(jnp.float32)
            + scale_o * ho[:, sl].astype(jnp.float32)
        )
    for n in range(half // cols):
        sl = pl.ds(n * cols, cols)
        partner(psend.at[n], precv.at[n], p_sem.at[n]).wait()
        outv[:, sl] = (pm[:, sl] + precv[n].astype(jnp.float32)).astype(jnp.bfloat16)
    result = out_ref.at[:, pl.ds(mine, half)]
    give = pltpu.make_async_remote_copy(
        src_ref=outv, dst_ref=result, send_sem=out_sem.at[0], recv_sem=out_sem.at[1],
        device_id=(1 - b, s, g), device_id_type=MESH,
    )
    keep = pltpu.make_async_copy(outv, result, out_sem.at[2])
    give.start()
    keep.start()

    @pl.when(active)
    def _():
        @pl.loop(0, blocks)
        def _(i):
            send_o(i, False)

    give.wait()
    keep.wait()


def local(
    hidden, queries, keys, values, output_weight, adapter_down_weight, adapter_up_weight,
    request_adapters, request_length,
):
    rows, width = queries.shape[1:]
    tokens = rows * 32
    bf16, f32 = jnp.bfloat16, jnp.float32
    dma = pltpu.SemaphoreType.DMA
    down = adapter_down_weight.transpose(1, 0, 2).reshape(width, -1)
    up = adapter_up_weight.reshape(-1, adapter_up_weight.shape[2])
    rank = down.shape[1]

    kbuf, vbuf, qbuf, hbuf = pl.pallas_call(
        scatter_kernel,
        out_shape=(
            jax.ShapeDtypeStruct((tokens, HS), bf16),
            jax.ShapeDtypeStruct((tokens, HS), bf16),
            jax.ShapeDtypeStruct((tokens // 2, HS), bf16),
            jax.ShapeDtypeStruct((rows, width), bf16),
        ),
        in_specs=[ANY] * 4,
        out_specs=(ANY,) * 4,
        scratch_shapes=[dma((30,)), dma((4,)), dma, dma((2,)), dma((2, 4))],
        compiler_params=pltpu.CompilerParams(has_side_effects=True),
        name="scatter_heads",
    )(queries, keys, values, hidden)

    steps = tokens // 2 // rows
    o = pl.pallas_call(
        attention_kernel,
        grid=(steps,),
        out_shape=jax.ShapeDtypeStruct((tokens // 2, HS), bf16),
        in_specs=[
            SMEM,
            pl.BlockSpec((rows, HS), lambda i: (i, 0)),
            pl.BlockSpec((tokens, HS), lambda i: (0, 0)),
            pl.BlockSpec((tokens, HS), lambda i: (0, 0)),
        ],
        out_specs=pl.BlockSpec((rows, HS), lambda i: (i, 0)),
        scratch_shapes=[
            pltpu.VMEM((tokens // BK + 1, rows, BK), f32),
            pltpu.VMEM((rows, HS), f32),
            pltpu.VMEM((rows, HS), f32),
            pltpu.VMEM((rows, HS), f32),
        ],
        compiler_params=pltpu.CompilerParams(vmem_limit_bytes=48 * 2**20),
        name="attend",
    )(request_length, qbuf, kbuf, vbuf)

    half = width
    cols = 256
    return pl.pallas_call(
        project_kernel,
        out_shape=jax.ShapeDtypeStruct((rows, 2 * half), bf16),
        in_specs=[SMEM, SMEM] + [ANY] * 6,
        out_specs=ANY,
        scratch_shapes=[
            pltpu.VMEM((2, rows, width), bf16),
            pltpu.VMEM((width, half), bf16),
            pltpu.VMEM((width, half), bf16),
            pltpu.VMEM((width, rank), bf16),
            pltpu.VMEM((rank, half), bf16),
            pltpu.VMEM((rows, half), bf16),
            pltpu.VMEM((rows, half), bf16),
            pltpu.VMEM((rows, width), bf16),
            pltpu.VMEM((rows, half), f32),
            pltpu.VMEM((half // cols, rows, cols), bf16),
            pltpu.VMEM((half // cols, rows, cols), bf16),
            pltpu.VMEM((rows, rank), bf16),
            pltpu.VMEM((rows, rank), bf16),
            pltpu.VMEM((rows, half), bf16),
            dma((6,)), dma((steps,)), dma, dma((2,)), dma((half // cols, 2)), dma((2,)), dma((3,)),
        ],
        compiler_params=pltpu.CompilerParams(
            has_side_effects=True, vmem_limit_bytes=48 * 2**20
        ),
        name="project",
    )(request_length, request_adapters, o, hidden, hbuf, output_weight, down, up)


def solution(mesh):
    return jax.shard_map(
        local,
        mesh=mesh,
        in_specs=(
            P("cfg", "seq", "head"),
            P("cfg", "seq", "head"),
            P("cfg", "seq", "head"),
            P("cfg", "seq", "head"),
            P("head", None),
            P(None, "head", None),
            P(None, None, "head"),
            P(),
            P(),
        ),
        out_specs=P("seq", "head"),
        check_vma=False,
    )
```

```python
import functools
import math

import jax
import jax.numpy as jnp
from jax import lax
from jax.experimental import pallas as pl
from jax.experimental.pallas import tpu as pltpu
from jax.sharding import PartitionSpec as P

MESH = pl.DeviceIdType.MESH
HS = 128
GUIDE = 5.0
BK = 1536
PAIR = 2
ANY = pl.BlockSpec(memory_space=pl.ANY)
SMEM = pl.BlockSpec(memory_space=pltpu.SMEM)


def place(head, branch):
    p = (head // 2) * 3 + head % 2
    return (p // 4) * 8 + branch * 4 + p % 4


def role(s):
    p = (s // 8) * 4 + s % 4
    active = jnp.logical_and(p % 3 < 2, p < 15)
    head = (p // 3) * 2 + p % 3
    return active, head, (s // 4) % 2


def signal(semaphore, *device):
    pl.semaphore_signal(semaphore, inc=1, device_id=device, device_id_type=MESH)


def scatter_kernel(
    q_ref, k_ref, v_ref, hid_ref, kbuf, vbuf, qbuf, hbuf,
    send_sem, kv_sem, q_sem, hid_sem, fwd_sem,
):
    b = lax.axis_index("cfg")
    s = lax.axis_index("seq")
    g = lax.axis_index("head")
    rows = q_ref.shape[1]
    heads = q_ref.shape[2] // HS
    half = hbuf.shape[1]
    active, _, branch = role(s)
    seqs = 32

    barrier = pltpu.get_barrier_semaphore()
    signal(barrier, 1 - b, s, g)

    @pl.when(active)
    def _():
        @pl.loop(0, seqs)
        def _(i):
            t = (s + i) % seqs

            @pl.when(jnp.logical_not(jnp.logical_and(t == s, branch == b)))
            def _():
                signal(barrier, branch, t, g)

    own = jnp.where(jnp.logical_and(active, branch == b), 1, 0)
    pl.semaphore_wait(barrier, 2 * heads + 1 - own)

    groups = kv_sem.shape[0]
    per = kbuf.shape[0] // groups

    other = pltpu.make_async_remote_copy(
        src_ref=hid_ref.at[0, :, pl.ds(pl.multiple_of((1 - b) * half, half), half)],
        dst_ref=hbuf,
        send_sem=hid_sem.at[0],
        recv_sem=hid_sem.at[1],
        device_id=(1 - b, s, g),
        device_id_type=MESH,
    )

    row0 = pl.multiple_of(s * rows, 32)
    qrow0 = pl.multiple_of((s // 2) * rows, 32)
    kind = (
        (k_ref, lambda: kbuf.at[pl.ds(row0, rows), :], kv_sem.at[s // (32 // groups)], 0),
        (v_ref, lambda: vbuf.at[pl.ds(row0, rows), :], kv_sem.at[s // (32 // groups)], 1),
        (q_ref, lambda: qbuf.at[pl.ds(qrow0, rows), :], q_sem, s % 2),
    )

    def each(i, act):
        h = (i + s) % heads
        target = place(h, b)
        for n, (src, dst, sem, core) in enumerate(kind):
            piece = src.at[0, :, pl.ds(pl.multiple_of(h * HS, HS), HS)]
            mine = jnp.logical_and(target == s, core == b)
            act(n, piece, dst(), sem, core, target, mine, i)

    def start(n, piece, dst, sem, core, target, mine, i):
        @pl.when(mine)
        def _():
            pltpu.make_async_copy(piece, dst, sem).start()

        @pl.when(jnp.logical_not(mine))
        def _():
            pltpu.make_async_remote_copy(
                src_ref=piece, dst_ref=dst, send_sem=send_sem.at[i * 3 + n], recv_sem=sem,
                device_id=(core, target, g), device_id_type=MESH,
            ).start()

    def finish(n, piece, dst, sem, core, target, mine, i):
        @pl.when(jnp.logical_not(mine))
        def _():
            pltpu.make_async_remote_copy(
                src_ref=piece, dst_ref=dst, send_sem=send_sem.at[i * 3 + n], recv_sem=sem,
                device_id=(core, target, g), device_id_type=MESH,
            ).wait_send()

    @pl.loop(0, heads)
    def _(i):
        each(i, start)

    other.start()

    def forward(buf, n):
        part = buf.at[pl.ds(n * per, per), :]
        return pltpu.make_async_remote_copy(
            src_ref=part, dst_ref=part, send_sem=fwd_sem.at[0, n], recv_sem=fwd_sem.at[1, n],
            device_id=(1 - b, s, g), device_id_type=MESH,
        )

    def landed(buf, sem):
        pltpu.make_async_copy(buf, buf, sem).wait()

    for core, (got, came) in enumerate(((kbuf, vbuf), (vbuf, kbuf))):

        @pl.when(jnp.logical_and(active, b == core))
        def _():
            for n in range(groups):
                landed(got.at[pl.ds(n * per, per), :], kv_sem.at[n])
                forward(got, n).start()
            for n in range(groups):
                forward(got, n).wait_send()
                forward(came, n).wait_recv()
            landed(qbuf, q_sem)

    @pl.loop(0, heads)
    def _(i):
        each(i, finish)

    other.wait()


def attention_kernel(len_ref, q_ref, k_ref, v_ref, o_ref, s_ref, m_ref, acc_ref):
    c = lax.axis_index("cfg")
    s = lax.axis_index("seq")
    active, _, _ = role(s)
    rows = q_ref.shape[0]
    piece = rows // PAIR
    tokens = k_ref.shape[0]
    factor = math.log2(math.e) / math.sqrt(HS)
    first = (2 * PAIR * pl.program_id(0) + c) * piece
    last = first + (2 * PAIR - 1) * piece - 1
    e0 = len_ref[0]
    e1 = e0 + len_ref[1]
    e2 = e1 + len_ref[2]

    def segment(pos):
        return (
            (pos >= e0).astype(jnp.int32)
            + (pos >= e1).astype(jnp.int32)
            + (pos >= e2).astype(jnp.int32)
        )

    @pl.when(active)
    def _():
        seg_first = segment(first)
        seg_last = segment(last)
        starts = (0, e0, e1, e2)
        ends = (e0, e1, e2, tokens)
        lo = jnp.int32(0)
        hi = jnp.int32(tokens)
        for n in range(4):
            lo = jnp.where(seg_first == n, starts[n], lo)
            hi = jnp.where(seg_last == n, ends[n], hi)
        base = (lo // 32) * 32
        blocks = pl.cdiv(hi - base, BK)
        single = seg_first == seg_last
        row = lax.broadcasted_iota(jnp.int32, (rows, 1), 0)
        seg_q = segment(first + row + (row // piece) * piece)
        m_ref[...] = jnp.full_like(m_ref, -1e30)

        def widest(x):
            out = m_ref[...]
            for n in range(BK // HS):
                out = jnp.maximum(out, x[:, n * HS : (n + 1) * HS])
            m_ref[...] = out

        def scores(at):
            return lax.dot_general(
                q_ref[...], k_ref[pl.ds(at, BK), :], (((1,), (1,)), ((), ())),
                preferred_element_type=jnp.float32,
            )

        @pl.loop(0, blocks)
        def _(n):
            logical = base + n * BK
            at = pl.multiple_of(jnp.minimum(logical, tokens - BK), 32)
            whole = jnp.logical_and(
                single, jnp.logical_and(logical >= lo, logical + BK <= hi)
            )

            @pl.when(whole)
            def _():
                score = scores(at)
                s_ref[n] = score
                widest(score)

            @pl.when(jnp.logical_not(whole))
            def _():
                pos = at + lax.broadcasted_iota(jnp.int32, (1, BK), 1)
                seg_k = jnp.where(pos >= logical, segment(pos), -1)
                score = jnp.where(seg_q == seg_k, scores(at), -jnp.inf)
                s_ref[n] = score
                widest(score)

        m_ref[...] = jnp.broadcast_to(
            jnp.max(m_ref[...], axis=1, keepdims=True), m_ref.shape
        )
        acc_ref[...] = jnp.zeros_like(acc_ref)

        @pl.loop(0, blocks)
        def _(n):
            at = pl.multiple_of(jnp.minimum(base + n * BK, tokens - BK), 32)
            top = m_ref[...]
            weight = jnp.concatenate(
                [
                    jnp.exp2((s_ref[n, :, j * HS : (j + 1) * HS] - top) * factor).astype(
                        jnp.bfloat16
                    )
                    for j in range(BK // HS)
                ],
                axis=1,
            )
            values = jnp.concatenate(
                [v_ref[pl.ds(at, BK), :], jnp.ones((BK, HS), jnp.bfloat16)], axis=1
            )
            acc_ref[...] += jnp.dot(weight, values, preferred_element_type=jnp.float32)

        o_ref[...] = (acc_ref[:, :HS] / acc_ref[:, HS:]).astype(o_ref.dtype)


def project_kernel(
    len_ref, ad_ref, o_ref, hid_ref, hbuf, w_ref, down_ref, up_ref, out_ref,
    att, wo, wm, downv, upv, hm, ho, dv, pm, psend, precv, isend, irecv, outv,
    load_sem, o_send, o_sem, att_sem, p_sem, i_sem, out_sem,
):
    b = lax.axis_index("cfg")
    s = lax.axis_index("seq")
    g = lax.axis_index("head")
    active, head, branch = role(s)
    rows, half = outv.shape
    width = 2 * half
    blocks = o_ref.shape[0] // rows
    mine = pl.multiple_of(b * half, half)

    barrier = pltpu.get_barrier_semaphore()
    signal(barrier, 1 - b, s, g)
    signal(barrier, b, s, 1 - g)

    @pl.loop(0, half // HS)
    def _(i):
        t = place((i + s) % (half // HS), b)

        @pl.when(jnp.logical_not(jnp.logical_and(t == s, s % 2 == b)))
        def _():
            signal(barrier, s % 2, t, g)

    own = jnp.where(jnp.logical_and(branch == b, s % 2 == b), 1, 0)
    pl.semaphore_wait(barrier, 2 + jnp.where(active, blocks - own, 0))

    loads = [
        (down_ref, downv),
        (w_ref.at[:, pl.ds(pl.multiple_of((1 - g) * width + b * half, half), half)], wo),
        (w_ref.at[:, pl.ds(pl.multiple_of(g * width + b * half, half), half)], wm),
        (up_ref.at[:, pl.ds(mine, half)], upv),
        (hid_ref.at[0, :, pl.ds(mine, half)], hm),
        (hbuf, ho),
    ]
    loads = [pltpu.make_async_copy(a, z, load_sem.at[n]) for n, (a, z) in enumerate(loads)]

    def send_o(i, go):
        j = 2 * i + b
        piece = o_ref.at[pl.ds(pl.multiple_of(i * rows, 32), rows), :]
        dst = att.at[branch, :, pl.ds(pl.multiple_of(head * HS, HS), HS)]
        here = jnp.logical_and(j == s, branch == b)

        @pl.when(here)
        def _():
            if go:
                pltpu.make_async_copy(piece, dst, o_sem).start()

        @pl.when(jnp.logical_not(here))
        def _():
            copy = pltpu.make_async_remote_copy(
                src_ref=piece, dst_ref=dst, send_sem=o_send.at[i], recv_sem=o_sem,
                device_id=(branch, j, g), device_id_type=MESH,
            )
            if go:
                copy.start()
            else:
                copy.wait_send()

    @pl.when(active)
    def _():
        @pl.loop(0, blocks)
        def _(i):
            send_o((i + s // 2) % blocks, True)

    for copy in loads:
        copy.start()

    pltpu.make_async_copy(att.at[b], att.at[b], o_sem).wait()
    swap = pltpu.make_async_remote_copy(
        src_ref=att.at[b], dst_ref=att.at[b], send_sem=att_sem.at[0], recv_sem=att_sem.at[1],
        device_id=(1 - b, s, g), device_id_type=MESH,
    )
    swap.start()
    swap.wait()
    dv[...] = (
        GUIDE * att[0].astype(jnp.float32) + (1.0 - GUIDE) * att[1].astype(jnp.float32)
    ).astype(jnp.bfloat16)

    def partner(src, dst, sems):
        return pltpu.make_async_remote_copy(
            src_ref=src, dst_ref=dst, send_sem=sems.at[0], recv_sem=sems.at[1],
            device_id=(b, s, 1 - g), device_id_type=MESH,
        )

    loads[0].wait()
    pos = s * rows + lax.broadcasted_iota(jnp.int32, (rows, 1), 0)
    e0 = len_ref[0]
    e1 = e0 + len_ref[1]
    e2 = e1 + len_ref[2]
    adapter = jnp.where(
        pos < e1,
        jnp.where(pos < e0, ad_ref[0], ad_ref[1]),
        jnp.where(pos < e2, ad_ref[2], ad_ref[3]),
    )
    rank = downv.shape[1] // 8
    lane = lax.broadcasted_iota(jnp.int32, (rows, downv.shape[1]), 1)
    picked = (lane // rank) == adapter
    inner = jnp.dot(dv[...], downv[...], preferred_element_type=jnp.float32)
    isend[...] = jnp.where(picked, inner, 0.0).astype(jnp.bfloat16)
    inner_copy = partner(isend, irecv, i_sem)
    inner_copy.start()

    cols = 256
    loads[1].wait()
    for n in range(half // cols):
        sl = pl.ds(n * cols, cols)
        psend[n] = jnp.dot(dv[...], wo[:, sl], preferred_element_type=jnp.float32).astype(jnp.bfloat16)
        partner(psend.at[n], precv.at[n], p_sem.at[n]).start()
    loads[2].wait()
    for n in range(half // cols):
        sl = pl.ds(n * cols, cols)
        pm[:, sl] = jnp.dot(dv[...], wm[:, sl], preferred_element_type=jnp.float32)
    for copy in loads[3:]:
        copy.wait()
    scale_m = jnp.where(b == 0, GUIDE, 1.0 - GUIDE).astype(jnp.float32)
    scale_o = jnp.where(b == 0, 1.0 - GUIDE, GUIDE).astype(jnp.float32)
    inner_copy.wait()
    both = jnp.where(
        picked, inner + irecv[...].astype(jnp.float32), 0.0
    ).astype(jnp.bfloat16)
    for n in range(half // cols):
        sl = pl.ds(n * cols, cols)
        pm[:, sl] += (
            jnp.dot(both, upv[:, sl], preferred_element_type=jnp.float32)
            + scale_m * hm[:, sl].astype(jnp.float32)
            + scale_o * ho[:, sl].astype(jnp.float32)
        )
    for n in range(half // cols):
        sl = pl.ds(n * cols, cols)
        partner(psend.at[n], precv.at[n], p_sem.at[n]).wait()
        outv[:, sl] = (pm[:, sl] + precv[n].astype(jnp.float32)).astype(jnp.bfloat16)
    result = out_ref.at[:, pl.ds(mine, half)]
    give = pltpu.make_async_remote_copy(
        src_ref=outv, dst_ref=result, send_sem=out_sem.at[0], recv_sem=out_sem.at[1],
        device_id=(1 - b, s, g), device_id_type=MESH,
    )
    keep = pltpu.make_async_copy(outv, result, out_sem.at[2])
    give.start()
    keep.start()

    @pl.when(active)
    def _():
        @pl.loop(0, blocks)
        def _(i):
            send_o(i, False)

    give.wait()
    keep.wait()


def local(
    hidden, queries, keys, values, output_weight, adapter_down_weight, adapter_up_weight,
    request_adapters, request_length,
):
    rows, width = queries.shape[1:]
    tokens = rows * 32
    bf16, f32 = jnp.bfloat16, jnp.float32
    dma = pltpu.SemaphoreType.DMA
    down = adapter_down_weight.transpose(1, 0, 2).reshape(width, -1)
    up = adapter_up_weight.reshape(-1, adapter_up_weight.shape[2])
    rank = down.shape[1]

    kbuf, vbuf, qbuf, hbuf = pl.pallas_call(
        scatter_kernel,
        out_shape=(
            jax.ShapeDtypeStruct((tokens, HS), bf16),
            jax.ShapeDtypeStruct((tokens, HS), bf16),
            jax.ShapeDtypeStruct((tokens // 2, HS), bf16),
            jax.ShapeDtypeStruct((rows, width), bf16),
        ),
        in_specs=[ANY] * 4,
        out_specs=(ANY,) * 4,
        scratch_shapes=[dma((30,)), dma((4,)), dma, dma((2,)), dma((2, 4))],
        compiler_params=pltpu.CompilerParams(has_side_effects=True, collective_id=1),
        name="scatter_heads",
    )(queries, keys, values, hidden)

    steps = tokens // 2 // rows
    tile = PAIR * rows
    o = pl.pallas_call(
        attention_kernel,
        grid=(steps // PAIR,),
        out_shape=jax.ShapeDtypeStruct((tokens // 2, HS), bf16),
        in_specs=[
            SMEM,
            pl.BlockSpec((tile, HS), lambda i: (i, 0)),
            pl.BlockSpec((tokens, HS), lambda i: (0, 0)),
            pl.BlockSpec((tokens, HS), lambda i: (0, 0)),
        ],
        out_specs=pl.BlockSpec((tile, HS), lambda i: (i, 0)),
        scratch_shapes=[
            pltpu.VMEM((pl.cdiv(tokens, BK), tile, BK), f32),
            pltpu.VMEM((tile, HS), f32),
            pltpu.VMEM((tile, 2 * HS), f32),
        ],
        compiler_params=pltpu.CompilerParams(vmem_limit_bytes=48 * 2**20),
        name="attend",
    )(request_length, qbuf, kbuf, vbuf)

    half = width
    cols = 256
    return pl.pallas_call(
        project_kernel,
        out_shape=jax.ShapeDtypeStruct((rows, 2 * half), bf16),
        in_specs=[SMEM, SMEM] + [ANY] * 6,
        out_specs=ANY,
        scratch_shapes=[
            pltpu.VMEM((2, rows, width), bf16),
            pltpu.VMEM((width, half), bf16),
            pltpu.VMEM((width, half), bf16),
            pltpu.VMEM((width, rank), bf16),
            pltpu.VMEM((rank, half), bf16),
            pltpu.VMEM((rows, half), bf16),
            pltpu.VMEM((rows, half), bf16),
            pltpu.VMEM((rows, width), bf16),
            pltpu.VMEM((rows, half), f32),
            pltpu.VMEM((half // cols, rows, cols), bf16),
            pltpu.VMEM((half // cols, rows, cols), bf16),
            pltpu.VMEM((rows, rank), bf16),
            pltpu.VMEM((rows, rank), bf16),
            pltpu.VMEM((rows, half), bf16),
            dma((6,)), dma((steps,)), dma, dma((2,)), dma((half // cols, 2)), dma((2,)), dma((3,)),
        ],
        compiler_params=pltpu.CompilerParams(
            has_side_effects=True, collective_id=2, vmem_limit_bytes=48 * 2**20
        ),
        name="project",
    )(request_length, request_adapters, o, hidden, hbuf, output_weight, down, up)


def solution(mesh):
    return jax.shard_map(
        local,
        mesh=mesh,
        in_specs=(
            P("cfg", "seq", "head"),
            P("cfg", "seq", "head"),
            P("cfg", "seq", "head"),
            P("cfg", "seq", "head"),
            P("head", None),
            P(None, "head", None),
            P(None, None, "head"),
            P(),
            P(),
        ),
        out_specs=P("seq", "head"),
        check_vma=False,
    )
```

```python
import functools
import math

import jax
import jax.numpy as jnp
from jax import lax
from jax.experimental import pallas as pl
from jax.experimental.pallas import tpu as pltpu
from jax.sharding import PartitionSpec as P

MESH = pl.DeviceIdType.MESH
HS = 128
GUIDE = 5.0
BK = 1536
PAIR = 2
PARTS = ((0, 64), (64, 48))
COLS = 512
ANY = pl.BlockSpec(memory_space=pl.ANY)
SMEM = pl.BlockSpec(memory_space=pltpu.SMEM)
VMEM = pl.BlockSpec(memory_space=pltpu.VMEM)


def place(head, branch):
    y = head // 2
    x = 2 * (head % 2) + (y + branch) % 2
    p = jnp.where(head < 8, y * 4 + x, jnp.where(head == 8, 1 - branch, 11 - branch))
    return (p // 4) * 8 + branch * 4 + p % 4


def role(s):
    x, y, branch = s % 4, s // 8, (s // 4) % 2
    p = y * 4 + x
    board = (x + y) % 2 == branch
    late = jnp.where(p == 1 - branch, 8, 9)
    active = jnp.logical_or(board, jnp.logical_or(p == 1 - branch, p == 11 - branch))
    return active, jnp.where(board, y * 2 + x // 2, late), branch


def signal(semaphore, *device):
    pl.semaphore_signal(semaphore, inc=1, device_id=device, device_id_type=MESH)


def scatter_kernel(
    q_ref, k_ref, v_ref, hid_ref, kbuf, vbuf, qbuf, hbuf,
    send_sem, kv_sem, q_sem, hid_sem, fwd_sem,
):
    b = lax.axis_index("cfg")
    s = lax.axis_index("seq")
    g = lax.axis_index("head")
    rows = q_ref.shape[1]
    heads = q_ref.shape[2] // HS
    half = hbuf.shape[0]
    active, _, branch = role(s)
    seqs = 32

    barrier = pltpu.get_barrier_semaphore()
    signal(barrier, 1 - b, s, g)

    @pl.when(active)
    def _():
        @pl.loop(0, seqs)
        def _(i):
            t = (s + i) % seqs

            @pl.when(jnp.logical_not(jnp.logical_and(t == s, branch == b)))
            def _():
                signal(barrier, branch, t, g)

    own = jnp.where(jnp.logical_and(active, branch == b), 1, 0)
    pl.semaphore_wait(barrier, 2 * heads + 1 - own)

    groups = kv_sem.shape[0]
    per = kbuf.shape[0] // groups

    other = pltpu.make_async_remote_copy(
        src_ref=hid_ref.at[0, pl.ds(pl.multiple_of((1 - b) * half, 16), half), :],
        dst_ref=hbuf,
        send_sem=hid_sem.at[0],
        recv_sem=hid_sem.at[1],
        device_id=(1 - b, s, g),
        device_id_type=MESH,
    )

    row0 = pl.multiple_of(s * rows, 32)
    qrow0 = pl.multiple_of((s // 2) * rows, 32)
    kind = (
        (k_ref, lambda: kbuf.at[pl.ds(row0, rows), :], kv_sem.at[s // (32 // groups)], 0),
        (v_ref, lambda: vbuf.at[pl.ds(row0, rows), :], kv_sem.at[s // (32 // groups)], 1),
        (q_ref, lambda: qbuf.at[pl.ds(qrow0, rows), :], q_sem, s % 2),
    )

    def each(i, act, kinds=(0, 1, 2)):
        h = (i + s) % heads
        target = place(h, b)
        for n in kinds:
            src, dst, sem, core = kind[n]
            piece = src.at[0, :, pl.ds(pl.multiple_of(h * HS, HS), HS)]
            mine = jnp.logical_and(target == s, core == b)
            act(n, piece, dst(), sem, core, target, mine, i)

    def start(n, piece, dst, sem, core, target, mine, i):
        @pl.when(mine)
        def _():
            pltpu.make_async_copy(piece, dst, sem).start()

        @pl.when(jnp.logical_not(mine))
        def _():
            pltpu.make_async_remote_copy(
                src_ref=piece, dst_ref=dst, send_sem=send_sem.at[i * 3 + n], recv_sem=sem,
                device_id=(core, target, g), device_id_type=MESH,
            ).start()

    def finish(n, piece, dst, sem, core, target, mine, i):
        @pl.when(jnp.logical_not(mine))
        def _():
            pltpu.make_async_remote_copy(
                src_ref=piece, dst_ref=dst, send_sem=send_sem.at[i * 3 + n], recv_sem=sem,
                device_id=(core, target, g), device_id_type=MESH,
            ).wait_send()

    for n in range(3):

        @pl.loop(0, heads)
        def _(i):
            each(i, start, (n,))

    other.start()

    def forward(buf, n):
        part = buf.at[pl.ds(n * per, per), :]
        return pltpu.make_async_remote_copy(
            src_ref=part, dst_ref=part, send_sem=fwd_sem.at[0, n], recv_sem=fwd_sem.at[1, n],
            device_id=(1 - b, s, g), device_id_type=MESH,
        )

    def landed(buf, sem):
        pltpu.make_async_copy(buf, buf, sem).wait()

    for core, (got, came) in enumerate(((kbuf, vbuf), (vbuf, kbuf))):

        @pl.when(jnp.logical_and(active, b == core))
        def _():
            for n in range(groups):
                landed(got.at[pl.ds(n * per, per), :], kv_sem.at[n])
                forward(got, n).start()
            for n in range(groups):
                forward(got, n).wait_send()
                forward(came, n).wait_recv()
            landed(qbuf, q_sem)

    @pl.loop(0, heads)
    def _(i):
        each(i, finish)

    other.wait()


def attention_kernel(len_ref, q_ref, k_ref, v_ref, o_ref, s_ref, m_ref, acc_ref):
    c = lax.axis_index("cfg")
    s = lax.axis_index("seq")
    active, _, _ = role(s)
    rows = acc_ref.shape[0]
    piece = rows // PAIR
    tokens = k_ref.shape[0]
    factor = math.log2(math.e) / math.sqrt(HS)
    e0 = len_ref[0]
    e1 = e0 + len_ref[1]
    e2 = e1 + len_ref[2]

    def segment(pos):
        return (
            (pos >= e0).astype(jnp.int32)
            + (pos >= e1).astype(jnp.int32)
            + (pos >= e2).astype(jnp.int32)
        )

    @pl.loop(0, jnp.where(active, q_ref.shape[0] // rows, 0))
    def _(tile):
        first = (2 * PAIR * tile + c) * piece
        last = first + (2 * PAIR - 1) * piece - 1
        own = pl.ds(pl.multiple_of(tile * rows, 32), rows)
        seg_first = segment(first)
        seg_last = segment(last)
        starts = (0, e0, e1, e2)
        ends = (e0, e1, e2, tokens)
        lo = jnp.int32(0)
        hi = jnp.int32(tokens)
        for n in range(4):
            lo = jnp.where(seg_first == n, starts[n], lo)
            hi = jnp.where(seg_last == n, ends[n], hi)
        base = (lo // 32) * 32
        blocks = pl.cdiv(hi - base, BK)
        single = seg_first == seg_last
        row = lax.broadcasted_iota(jnp.int32, (rows, 1), 0)
        seg_q = segment(first + row + (row // piece) * piece)
        m_ref[...] = jnp.full_like(m_ref, -1e30)

        def widest(x):
            out = m_ref[...]
            for n in range(BK // HS):
                out = jnp.maximum(out, x[:, n * HS : (n + 1) * HS])
            m_ref[...] = out

        def scores(at):
            return lax.dot_general(
                q_ref[own, :], k_ref[pl.ds(at, BK), :], (((1,), (1,)), ((), ())),
                preferred_element_type=jnp.float32,
            )

        @pl.loop(0, blocks)
        def _(n):
            logical = base + n * BK
            at = pl.multiple_of(jnp.minimum(logical, tokens - BK), 32)
            whole = jnp.logical_and(
                single, jnp.logical_and(logical >= lo, logical + BK <= hi)
            )

            @pl.when(whole)
            def _():
                score = scores(at)
                s_ref[n] = score
                widest(score)

            @pl.when(jnp.logical_not(whole))
            def _():
                pos = at + lax.broadcasted_iota(jnp.int32, (1, BK), 1)
                seg_k = jnp.where(pos >= logical, segment(pos), -1)
                score = jnp.where(seg_q == seg_k, scores(at), -jnp.inf)
                s_ref[n] = score
                widest(score)

        m_ref[...] = jnp.broadcast_to(
            jnp.max(m_ref[...], axis=1, keepdims=True), m_ref.shape
        )
        acc_ref[...] = jnp.zeros_like(acc_ref)

        @pl.loop(0, blocks)
        def _(n):
            at = pl.multiple_of(jnp.minimum(base + n * BK, tokens - BK), 32)
            top = m_ref[...]
            weight = jnp.concatenate(
                [
                    jnp.exp2((s_ref[n, :, j * HS : (j + 1) * HS] - top) * factor).astype(
                        jnp.bfloat16
                    )
                    for j in range(BK // HS)
                ],
                axis=1,
            )
            values = jnp.concatenate(
                [v_ref[pl.ds(at, BK), :], jnp.ones((BK, HS), jnp.bfloat16)], axis=1
            )
            acc_ref[...] += jnp.dot(weight, values, preferred_element_type=jnp.float32)

        o_ref[own, :] = (acc_ref[:, :HS] / acc_ref[:, HS:]).astype(o_ref.dtype)


def project_kernel(
    len_ref, ad_ref, o_ref, hid_ref, hbuf, w_ref, down_ref, up_ref, out_ref,
    att, wo, wm, downv, upv, hm, ho, dv, inner, picked, pm, psend, precv, isend, irecv, outv,
    load_sem, o_send, o_sem, p_sem, i_sem, out_sem,
):
    b = lax.axis_index("cfg")
    s = lax.axis_index("seq")
    g = lax.axis_index("head")
    active, head, branch = role(s)
    half, width = outv.shape
    rows = 2 * half
    heads = att.shape[2] // HS
    blocks = o_ref.shape[0] // rows
    chunks = range(width // COLS)
    top = pl.multiple_of(b * half, 16)

    barrier = pltpu.get_barrier_semaphore()
    signal(barrier, 1 - b, s, g)
    signal(barrier, b, s, 1 - g)

    for origin in range(2):

        @pl.loop(0, heads)
        def _(i):
            t = place((i + s) % heads, origin)

            @pl.when(jnp.logical_not(jnp.logical_and(t == s, s % 2 == b)))
            def _():
                signal(barrier, s % 2, t, g)

    own = jnp.where(s % 2 == b, 1, 0)
    pl.semaphore_wait(barrier, 2 + jnp.where(active, 2 * blocks - own, 0))

    def send_o(i, n, core, go):
        j = 2 * i + b
        first, count = PARTS[n]
        piece = o_ref.at[pl.ds(pl.multiple_of(i * rows + core * half + first, 16), count), :]
        dst = att.at[branch, pl.ds(first, count), pl.ds(pl.multiple_of(head * HS, HS), HS)]
        here = jnp.logical_and(j == s, core == b)

        @pl.when(here)
        def _():
            if go:
                pltpu.make_async_copy(piece, dst, o_sem.at[n]).start()

        @pl.when(jnp.logical_not(here))
        def _():
            copy = pltpu.make_async_remote_copy(
                src_ref=piece, dst_ref=dst, send_sem=o_send.at[n, core, i], recv_sem=o_sem.at[n],
                device_id=(core, j, g), device_id_type=MESH,
            )
            if go:
                copy.start()
            else:
                copy.wait_send()

    @pl.when(active)
    def _():
        for n in range(len(PARTS)):

            @pl.loop(0, blocks)
            def _(i):
                for core in range(2):
                    send_o((i + s // 2) % blocks, n, core, True)

    loads = [
        (down_ref, downv),
        (w_ref.at[:, pl.ds(pl.multiple_of((1 - g) * width, width), width)], wo),
        (w_ref.at[:, pl.ds(pl.multiple_of(g * width, width), width)], wm),
        (up_ref, upv),
        (hid_ref.at[0, pl.ds(top, half), :], hm),
        (hbuf, ho),
    ]
    loads = [pltpu.make_async_copy(a, z, load_sem.at[n]) for n, (a, z) in enumerate(loads)]
    for copy in loads:
        copy.start()

    def partner(src, dst, sems):
        return pltpu.make_async_remote_copy(
            src_ref=src, dst_ref=dst, send_sem=sems.at[0], recv_sem=sems.at[1],
            device_id=(b, s, 1 - g), device_id_type=MESH,
        )

    rank = downv.shape[0] // 8
    pos = s * rows + b * half + lax.broadcasted_iota(jnp.int32, picked.shape, 0)
    lane = lax.broadcasted_iota(jnp.int32, picked.shape, 1)
    e0 = len_ref[0]
    e1 = e0 + len_ref[1]
    e2 = e1 + len_ref[2]
    adapter = jnp.where(
        pos < e1,
        jnp.where(pos < e0, ad_ref[0], ad_ref[1]),
        jnp.where(pos < e2, ad_ref[2], ad_ref[3]),
    )
    picked[...] = ((lane // rank) == adapter).astype(jnp.float32)
    for copy in loads:
        copy.wait()
    scale_m = jnp.where(b == 0, GUIDE, 1.0 - GUIDE).astype(jnp.float32)
    scale_o = jnp.where(b == 0, 1.0 - GUIDE, GUIDE).astype(jnp.float32)
    pm[...] = scale_m * hm[...].astype(jnp.float32) + scale_o * ho[...].astype(jnp.float32)

    def column(c):
        return slice(c * COLS, (c + 1) * COLS)

    for n, (first, count) in enumerate(PARTS):
        sl = slice(first, first + count)
        came = att.at[:, pl.ds(first, count), :]
        pltpu.make_async_copy(came, came, o_sem.at[n]).wait()
        dv[sl, :] = (
            GUIDE * att[0, sl, :].astype(jnp.float32)
            + (1.0 - GUIDE) * att[1, sl, :].astype(jnp.float32)
        ).astype(jnp.bfloat16)
        for c in chunks:
            psend[c, sl, :] = jnp.dot(
                dv[sl, :], wo[:, column(c)], preferred_element_type=jnp.float32
            ).astype(jnp.bfloat16)
            partner(psend.at[c, sl, :], precv.at[c, sl, :], p_sem.at[n, c]).start()
            if c == 0:
                inner[sl, :] = (
                    lax.dot_general(
                        dv[sl, :], downv[...], (((1,), (1,)), ((), ())),
                        preferred_element_type=jnp.float32,
                    )
                    * picked[sl, :]
                )
                isend[sl, :] = inner[sl, :].astype(jnp.bfloat16)
                partner(isend.at[sl, :], irecv.at[sl, :], i_sem.at[n]).start()
    for c in chunks:
        pm[:, column(c)] += jnp.dot(
            dv[...], wm[:, column(c)], preferred_element_type=jnp.float32
        )
    for n, (first, count) in enumerate(PARTS):
        sl = slice(first, first + count)
        partner(isend.at[sl, :], irecv.at[sl, :], i_sem.at[n]).wait()
    both = (inner[...] + irecv[...].astype(jnp.float32)).astype(jnp.bfloat16)
    for c in chunks:
        pm[:, column(c)] += jnp.dot(both, upv[:, column(c)], preferred_element_type=jnp.float32)
    last = []
    for n, (first, count) in enumerate(PARTS):
        sl = slice(first, first + count)
        for c in chunks:
            partner(psend.at[c, sl, :], precv.at[c, sl, :], p_sem.at[n, c]).wait()
            outv[sl, column(c)] = (
                pm[sl, column(c)] + precv[c, sl, :].astype(jnp.float32)
            ).astype(jnp.bfloat16)
            piece = outv.at[sl, pl.ds(c * COLS, COLS)]
            result = out_ref.at[pl.ds(pl.multiple_of(top + first, 16), count), pl.ds(c * COLS, COLS)]
            last.append(
                pltpu.make_async_remote_copy(
                    src_ref=piece, dst_ref=result,
                    send_sem=out_sem.at[n, c, 0], recv_sem=out_sem.at[n, c, 1],
                    device_id=(1 - b, s, g), device_id_type=MESH,
                )
            )
            last.append(pltpu.make_async_copy(piece, result, out_sem.at[n, c, 2]))
            last[-2].start()
            last[-1].start()

    @pl.when(active)
    def _():
        for n in range(len(PARTS)):

            @pl.loop(0, blocks)
            def _(i):
                for core in range(2):
                    send_o(i, n, core, False)

    for copy in last:
        copy.wait()


def local(
    hidden, queries, keys, values, output_weight, adapter_down_weight, adapter_up_weight,
    request_adapters, request_length,
):
    rows, width = queries.shape[1:]
    tokens = rows * 32
    bf16, f32 = jnp.bfloat16, jnp.float32
    dma = pltpu.SemaphoreType.DMA
    down = adapter_down_weight.transpose(0, 2, 1).reshape(-1, width)
    up = adapter_up_weight.reshape(-1, adapter_up_weight.shape[2])
    rank = up.shape[0]

    kbuf, vbuf, qbuf, hbuf = pl.pallas_call(
        scatter_kernel,
        out_shape=(
            jax.ShapeDtypeStruct((tokens, HS), bf16),
            jax.ShapeDtypeStruct((tokens, HS), bf16),
            jax.ShapeDtypeStruct((tokens // 2, HS), bf16),
            jax.ShapeDtypeStruct((rows // 2, 2 * width), bf16),
        ),
        in_specs=[ANY] * 4,
        out_specs=(ANY,) * 4,
        scratch_shapes=[dma((30,)), dma((4,)), dma, dma((2,)), dma((2, 4))],
        compiler_params=pltpu.CompilerParams(
            has_side_effects=True, collective_id=1, vmem_limit_bytes=2**20
        ),
        name="scatter_heads",
    )(queries, keys, values, hidden)

    steps = tokens // 2 // rows
    tile = PAIR * rows
    o = pl.pallas_call(
        attention_kernel,
        out_shape=jax.ShapeDtypeStruct((tokens // 2, HS), bf16),
        in_specs=[SMEM, VMEM, VMEM, VMEM],
        out_specs=VMEM,
        scratch_shapes=[
            pltpu.VMEM((pl.cdiv(tokens, BK), tile, BK), f32),
            pltpu.VMEM((tile, HS), f32),
            pltpu.VMEM((tile, 2 * HS), f32),
        ],
        compiler_params=pltpu.CompilerParams(vmem_limit_bytes=40 * 2**20),
        name="attend",
    )(request_length, qbuf, kbuf, vbuf)

    half = rows // 2
    chunks = 2 * width // COLS
    parts = len(PARTS)
    return pl.pallas_call(
        project_kernel,
        out_shape=jax.ShapeDtypeStruct((rows, 2 * width), bf16),
        in_specs=[SMEM, SMEM] + [ANY] * 6,
        out_specs=ANY,
        scratch_shapes=[
            pltpu.VMEM((2, half, width), bf16),
            pltpu.VMEM((width, 2 * width), bf16),
            pltpu.VMEM((width, 2 * width), bf16),
            pltpu.VMEM((rank, width), bf16),
            pltpu.VMEM((rank, 2 * width), bf16),
            pltpu.VMEM((half, 2 * width), bf16),
            pltpu.VMEM((half, 2 * width), bf16),
            pltpu.VMEM((half, width), bf16),
            pltpu.VMEM((half, rank), f32),
            pltpu.VMEM((half, rank), f32),
            pltpu.VMEM((half, 2 * width), f32),
            pltpu.VMEM((chunks, half, COLS), bf16),
            pltpu.VMEM((chunks, half, COLS), bf16),
            pltpu.VMEM((half, rank), bf16),
            pltpu.VMEM((half, rank), bf16),
            pltpu.VMEM((half, 2 * width), bf16),
            dma((6,)), dma((parts, 2, steps)), dma((parts,)),
            dma((parts, chunks, 2)), dma((parts, 2)), dma((parts, chunks, 3)),
        ],
        compiler_params=pltpu.CompilerParams(
            has_side_effects=True, collective_id=2, vmem_limit_bytes=48 * 2**20
        ),
        name="project",
    )(request_length, request_adapters, o, hidden, hbuf, output_weight, down, up)


def solution(mesh):
    return jax.shard_map(
        local,
        mesh=mesh,
        in_specs=(
            P("cfg", "seq", "head"),
            P("cfg", "seq", "head"),
            P("cfg", "seq", "head"),
            P("cfg", "seq", "head"),
            P("head", None),
            P(None, "head", None),
            P(None, None, "head"),
            P(),
            P(),
        ),
        out_specs=P("seq", "head"),
        check_vma=False,
    )
```

```python
import functools
import math

import jax
import jax.numpy as jnp
from jax import lax
from jax.experimental import pallas as pl
from jax.experimental.pallas import tpu as pltpu
from jax.sharding import PartitionSpec as P

MESH = pl.DeviceIdType.MESH
HS = 128
GUIDE = 5.0
BK = 1536
PAIR = 2
PARTS = ((0, 64), (64, 48))
COLS = 512
ANY = pl.BlockSpec(memory_space=pl.ANY)
SMEM = pl.BlockSpec(memory_space=pltpu.SMEM)
VMEM = pl.BlockSpec(memory_space=pltpu.VMEM)


def place(head, branch):
    y = head // 2
    x = 2 * (head % 2) + (y + branch) % 2
    p = jnp.where(head < 8, y * 4 + x, jnp.where(head == 8, 1 - branch, 11 - branch))
    return (p // 4) * 8 + branch * 4 + p % 4


def role(s):
    x, y, branch = s % 4, s // 8, (s // 4) % 2
    p = y * 4 + x
    board = (x + y) % 2 == branch
    late = jnp.where(p == 1 - branch, 8, 9)
    active = jnp.logical_or(board, jnp.logical_or(p == 1 - branch, p == 11 - branch))
    return active, jnp.where(board, y * 2 + x // 2, late), branch


def signal(semaphore, *device):
    pl.semaphore_signal(semaphore, inc=1, device_id=device, device_id_type=MESH)


def scatter_kernel(
    q_ref, k_ref, v_ref, hid_ref, kbuf, vbuf, qbuf, hbuf,
    send_sem, kv_sem, q_sem, hid_sem, fwd_sem,
):
    b = lax.axis_index("cfg")
    s = lax.axis_index("seq")
    g = lax.axis_index("head")
    rows = q_ref.shape[1]
    heads = q_ref.shape[2] // HS
    half = hbuf.shape[0]
    active, _, branch = role(s)
    seqs = 32

    barrier = pltpu.get_barrier_semaphore()
    signal(barrier, 1 - b, s, g)

    @pl.when(active)
    def _():
        @pl.loop(0, seqs)
        def _(i):
            t = (s + i) % seqs

            @pl.when(jnp.logical_not(jnp.logical_and(t == s, branch == b)))
            def _():
                signal(barrier, branch, t, g)

    own = jnp.where(jnp.logical_and(active, branch == b), 1, 0)
    pl.semaphore_wait(barrier, 2 * heads + 1 - own)

    groups = kv_sem.shape[0]
    per = kbuf.shape[0] // groups

    other = pltpu.make_async_remote_copy(
        src_ref=hid_ref.at[0, pl.ds(pl.multiple_of((1 - b) * half, 16), half), :],
        dst_ref=hbuf,
        send_sem=hid_sem.at[0],
        recv_sem=hid_sem.at[1],
        device_id=(1 - b, s, g),
        device_id_type=MESH,
    )

    row0 = pl.multiple_of(s * rows, 32)
    qrow0 = pl.multiple_of((s // 2) * rows, 32)
    kind = (
        (k_ref, lambda: kbuf.at[pl.ds(row0, rows), :], kv_sem.at[s // (32 // groups)], 0),
        (v_ref, lambda: vbuf.at[pl.ds(row0, rows), :], kv_sem.at[s // (32 // groups)], 1),
        (q_ref, lambda: qbuf.at[pl.ds(qrow0, rows), :], q_sem, s % 2),
    )

    def each(i, act, kinds=(0, 1, 2)):
        h = (i + s) % heads
        target = place(h, b)
        for n in kinds:
            src, dst, sem, core = kind[n]
            piece = src.at[0, :, pl.ds(pl.multiple_of(h * HS, HS), HS)]
            mine = jnp.logical_and(target == s, core == b)
            act(n, piece, dst(), sem, core, target, mine, i)

    def start(n, piece, dst, sem, core, target, mine, i):
        @pl.when(mine)
        def _():
            pltpu.make_async_copy(piece, dst, sem).start()

        @pl.when(jnp.logical_not(mine))
        def _():
            pltpu.make_async_remote_copy(
                src_ref=piece, dst_ref=dst, send_sem=send_sem.at[i * 3 + n], recv_sem=sem,
                device_id=(core, target, g), device_id_type=MESH,
            ).start()

    def finish(n, piece, dst, sem, core, target, mine, i):
        @pl.when(jnp.logical_not(mine))
        def _():
            pltpu.make_async_remote_copy(
                src_ref=piece, dst_ref=dst, send_sem=send_sem.at[i * 3 + n], recv_sem=sem,
                device_id=(core, target, g), device_id_type=MESH,
            ).wait_send()

    for n in range(3):

        @pl.loop(0, heads)
        def _(i):
            each(i, start, (n,))

    other.start()

    def forward(buf, n):
        part = buf.at[pl.ds(n * per, per), :]
        return pltpu.make_async_remote_copy(
            src_ref=part, dst_ref=part, send_sem=fwd_sem.at[0, n], recv_sem=fwd_sem.at[1, n],
            device_id=(1 - b, s, g), device_id_type=MESH,
        )

    def landed(buf, sem):
        pltpu.make_async_copy(buf, buf, sem).wait()

    for core, (got, came) in enumerate(((kbuf, vbuf), (vbuf, kbuf))):

        @pl.when(jnp.logical_and(active, b == core))
        def _():
            for n in range(groups):
                landed(got.at[pl.ds(n * per, per), :], kv_sem.at[n])
                forward(got, n).start()
            for n in range(groups):
                forward(got, n).wait_send()
                forward(came, n).wait_recv()
            landed(qbuf, q_sem)

    @pl.loop(0, heads)
    def _(i):
        each(i, finish)

    other.wait()


def attention_kernel(len_ref, q_ref, k_ref, v_ref, o_ref, s_ref, m_ref, acc_ref):
    c = lax.axis_index("cfg")
    s = lax.axis_index("seq")
    active, _, _ = role(s)
    rows = acc_ref.shape[0]
    piece = rows // PAIR
    tokens = k_ref.shape[0]
    factor = math.log2(math.e) / math.sqrt(HS)
    e0 = len_ref[0]
    e1 = e0 + len_ref[1]
    e2 = e1 + len_ref[2]

    def segment(pos):
        return (
            (pos >= e0).astype(jnp.int32)
            + (pos >= e1).astype(jnp.int32)
            + (pos >= e2).astype(jnp.int32)
        )

    @pl.loop(0, jnp.where(active, q_ref.shape[0] // rows, 0))
    def _(tile):
        first = (2 * PAIR * tile + c) * piece
        last = first + (2 * PAIR - 1) * piece - 1
        own = pl.ds(pl.multiple_of(tile * rows, 32), rows)
        seg_first = segment(first)
        seg_last = segment(last)
        starts = (0, e0, e1, e2)
        ends = (e0, e1, e2, tokens)
        lo = jnp.int32(0)
        hi = jnp.int32(tokens)
        for n in range(4):
            lo = jnp.where(seg_first == n, starts[n], lo)
            hi = jnp.where(seg_last == n, ends[n], hi)
        base = (lo // 32) * 32
        blocks = pl.cdiv(hi - base, BK)
        single = seg_first == seg_last
        row = lax.broadcasted_iota(jnp.int32, (rows, 1), 0)
        seg_q = segment(first + row + (row // piece) * piece)
        m_ref[...] = jnp.full_like(m_ref, -1e30)

        def widest(x):
            out = m_ref[...]
            for n in range(BK // HS):
                out = jnp.maximum(out, x[:, n * HS : (n + 1) * HS])
            m_ref[...] = out

        def scores(at):
            return lax.dot_general(
                q_ref[own, :], k_ref[pl.ds(at, BK), :], (((1,), (1,)), ((), ())),
                preferred_element_type=jnp.float32,
            )

        @pl.loop(0, blocks)
        def _(n):
            logical = base + n * BK
            at = pl.multiple_of(jnp.minimum(logical, tokens - BK), 32)
            whole = jnp.logical_and(
                single, jnp.logical_and(logical >= lo, logical + BK <= hi)
            )

            @pl.when(whole)
            def _():
                score = scores(at)
                s_ref[n] = score
                widest(score)

            @pl.when(jnp.logical_not(whole))
            def _():
                pos = at + lax.broadcasted_iota(jnp.int32, (1, BK), 1)
                seg_k = jnp.where(pos >= logical, segment(pos), -1)
                score = jnp.where(seg_q == seg_k, scores(at), -jnp.inf)
                s_ref[n] = score
                widest(score)

        m_ref[...] = jnp.broadcast_to(
            jnp.max(m_ref[...], axis=1, keepdims=True), m_ref.shape
        )
        acc_ref[...] = jnp.zeros_like(acc_ref)

        @pl.loop(0, blocks)
        def _(n):
            at = pl.multiple_of(jnp.minimum(base + n * BK, tokens - BK), 32)
            top = m_ref[...]
            weight = jnp.concatenate(
                [
                    jnp.exp2((s_ref[n, :, j * HS : (j + 1) * HS] - top) * factor).astype(
                        jnp.bfloat16
                    )
                    for j in range(BK // HS)
                ],
                axis=1,
            )
            values = jnp.concatenate(
                [v_ref[pl.ds(at, BK), :], jnp.ones((BK, HS), jnp.bfloat16)], axis=1
            )
            acc_ref[...] += jnp.dot(weight, values, preferred_element_type=jnp.float32)

        o_ref[own, :] = (acc_ref[:, :HS] / acc_ref[:, HS:]).astype(o_ref.dtype)


def project_kernel(
    len_ref, ad_ref, o_ref, hid_ref, hbuf, w_ref, down_ref, up_ref, out_ref,
    att, wo, wm, downv, upv, hm, ho, dv, inner, picked, pm, psend, precv, isend, irecv, outv,
    load_sem, o_send, o_sem, p_sem, i_sem, out_sem,
):
    b = lax.axis_index("cfg")
    s = lax.axis_index("seq")
    g = lax.axis_index("head")
    active, head, branch = role(s)
    half, width = outv.shape
    rows = 2 * half
    heads = att.shape[2] // HS
    blocks = o_ref.shape[0] // rows
    chunks = range(width // COLS)
    top = pl.multiple_of(b * half, 16)

    barrier = pltpu.get_barrier_semaphore()
    signal(barrier, 1 - b, s, g)
    signal(barrier, b, s, 1 - g)

    for origin in range(2):

        @pl.loop(0, heads)
        def _(i):
            t = place((i + s) % heads, origin)

            @pl.when(jnp.logical_not(jnp.logical_and(t == s, s % 2 == b)))
            def _():
                signal(barrier, s % 2, t, g)

    own = jnp.where(s % 2 == b, 1, 0)
    pl.semaphore_wait(barrier, 2 + jnp.where(active, 2 * blocks - own, 0))

    def send_o(i, n, core, go):
        j = 2 * i + b
        first, count = PARTS[n]
        piece = o_ref.at[pl.ds(pl.multiple_of(i * rows + core * half + first, 16), count), :]
        dst = att.at[branch, pl.ds(first, count), pl.ds(pl.multiple_of(head * HS, HS), HS)]
        here = jnp.logical_and(j == s, core == b)

        @pl.when(here)
        def _():
            if go:
                pltpu.make_async_copy(piece, dst, o_sem.at[n]).start()

        @pl.when(jnp.logical_not(here))
        def _():
            copy = pltpu.make_async_remote_copy(
                src_ref=piece, dst_ref=dst, send_sem=o_send.at[n, core, i], recv_sem=o_sem.at[n],
                device_id=(core, j, g), device_id_type=MESH,
            )
            if go:
                copy.start()
            else:
                copy.wait_send()

    @pl.when(active)
    def _():
        for n in range(len(PARTS)):

            @pl.loop(0, blocks)
            def _(i):
                for core in range(2):
                    send_o((i + s // 2) % blocks, n, core, True)

    loads = [
        (down_ref, downv),
        (w_ref.at[:, pl.ds(pl.multiple_of((1 - g) * width, width), width)], wo),
        (w_ref.at[:, pl.ds(pl.multiple_of(g * width, width), width)], wm),
        (up_ref, upv),
        (hid_ref.at[0, pl.ds(top, half), :], hm),
        (hbuf, ho),
    ]
    loads = [pltpu.make_async_copy(a, z, load_sem.at[n]) for n, (a, z) in enumerate(loads)]
    for copy in loads:
        copy.start()

    def partner(src, dst, sems):
        return pltpu.make_async_remote_copy(
            src_ref=src, dst_ref=dst, send_sem=sems.at[0], recv_sem=sems.at[1],
            device_id=(b, s, 1 - g), device_id_type=MESH,
        )

    rank = downv.shape[0] // 8
    pos = s * rows + b * half + lax.broadcasted_iota(jnp.int32, picked.shape, 0)
    lane = lax.broadcasted_iota(jnp.int32, picked.shape, 1)
    e0 = len_ref[0]
    e1 = e0 + len_ref[1]
    e2 = e1 + len_ref[2]
    adapter = jnp.where(
        pos < e1,
        jnp.where(pos < e0, ad_ref[0], ad_ref[1]),
        jnp.where(pos < e2, ad_ref[2], ad_ref[3]),
    )
    picked[...] = ((lane // rank) == adapter).astype(jnp.float32)
    for copy in loads:
        copy.wait()
    scale_m = jnp.where(b == 0, GUIDE, 1.0 - GUIDE).astype(jnp.float32)
    scale_o = jnp.where(b == 0, 1.0 - GUIDE, GUIDE).astype(jnp.float32)
    pm[...] = scale_m * hm[...].astype(jnp.float32) + scale_o * ho[...].astype(jnp.float32)

    def column(c):
        return slice(c * COLS, (c + 1) * COLS)

    for n, (first, count) in enumerate(PARTS):
        sl = slice(first, first + count)
        came = att.at[:, pl.ds(first, count), :]
        pltpu.make_async_copy(came, came, o_sem.at[n]).wait()
        dv[sl, :] = (
            GUIDE * att[0, sl, :].astype(jnp.float32)
            + (1.0 - GUIDE) * att[1, sl, :].astype(jnp.float32)
        ).astype(jnp.bfloat16)
        for c in chunks:
            psend[c, sl, :] = jnp.dot(
                dv[sl, :], wo[:, column(c)], preferred_element_type=jnp.float32
            ).astype(jnp.bfloat16)
            partner(psend.at[c, sl, :], precv.at[c, sl, :], p_sem.at[n, c]).start()
            if c == 0:
                inner[sl, :] = (
                    lax.dot_general(
                        dv[sl, :], downv[...], (((1,), (1,)), ((), ())),
                        preferred_element_type=jnp.float32,
                    )
                    * picked[sl, :]
                )
                isend[sl, :] = inner[sl, :].astype(jnp.bfloat16)
                partner(isend.at[sl, :], irecv.at[sl, :], i_sem.at[n]).start()
    for c in chunks:
        pm[:, column(c)] += jnp.dot(
            dv[...], wm[:, column(c)], preferred_element_type=jnp.float32
        )
    for n, (first, count) in enumerate(PARTS):
        sl = slice(first, first + count)
        partner(isend.at[sl, :], irecv.at[sl, :], i_sem.at[n]).wait()
    both = (inner[...] + irecv[...].astype(jnp.float32)).astype(jnp.bfloat16)
    for c in chunks:
        pm[:, column(c)] += jnp.dot(both, upv[:, column(c)], preferred_element_type=jnp.float32)
    last = []
    for n, (first, count) in enumerate(PARTS):
        sl = slice(first, first + count)
        for c in chunks:
            partner(psend.at[c, sl, :], precv.at[c, sl, :], p_sem.at[n, c]).wait()
            outv[sl, column(c)] = (
                pm[sl, column(c)] + precv[c, sl, :].astype(jnp.float32)
            ).astype(jnp.bfloat16)
            piece = outv.at[sl, pl.ds(c * COLS, COLS)]
            result = out_ref.at[pl.ds(pl.multiple_of(top + first, 16), count), pl.ds(c * COLS, COLS)]
            last.append(
                pltpu.make_async_remote_copy(
                    src_ref=piece, dst_ref=result,
                    send_sem=out_sem.at[n, c, 0], recv_sem=out_sem.at[n, c, 1],
                    device_id=(1 - b, s, g), device_id_type=MESH,
                )
            )
            last.append(pltpu.make_async_copy(piece, result, out_sem.at[n, c, 2]))
            last[-2].start()
            last[-1].start()

    @pl.when(active)
    def _():
        for n in range(len(PARTS)):

            @pl.loop(0, blocks)
            def _(i):
                for core in range(2):
                    send_o(i, n, core, False)

    for copy in last:
        copy.wait()


def local(
    hidden, queries, keys, values, output_weight, adapter_down_weight, adapter_up_weight,
    request_adapters, request_length,
):
    rows, width = queries.shape[1:]
    tokens = rows * 32
    bf16, f32 = jnp.bfloat16, jnp.float32
    dma = pltpu.SemaphoreType.DMA
    down = adapter_down_weight.transpose(0, 2, 1).reshape(-1, width)
    up = adapter_up_weight.reshape(-1, adapter_up_weight.shape[2])
    rank = up.shape[0]

    kbuf, vbuf, qbuf, hbuf = pl.pallas_call(
        scatter_kernel,
        out_shape=(
            jax.ShapeDtypeStruct((tokens, HS), bf16),
            jax.ShapeDtypeStruct((tokens, HS), bf16),
            jax.ShapeDtypeStruct((tokens // 2, HS), bf16),
            jax.ShapeDtypeStruct((rows // 2, 2 * width), bf16),
        ),
        in_specs=[ANY] * 4,
        out_specs=(ANY,) * 4,
        scratch_shapes=[dma((30,)), dma((4,)), dma, dma((2,)), dma((2, 4))],
        compiler_params=pltpu.CompilerParams(
            has_side_effects=True, collective_id=1, vmem_limit_bytes=2**20
        ),
        name="scatter_heads",
    )(*(pltpu.with_memory_space_constraint(x, pltpu.HBM) for x in (queries, keys, values, hidden)))

    steps = tokens // 2 // rows
    tile = PAIR * rows
    o = pl.pallas_call(
        attention_kernel,
        out_shape=jax.ShapeDtypeStruct((tokens // 2, HS), bf16),
        in_specs=[SMEM, VMEM, VMEM, VMEM],
        out_specs=VMEM,
        scratch_shapes=[
            pltpu.VMEM((pl.cdiv(tokens, BK), tile, BK), f32),
            pltpu.VMEM((tile, HS), f32),
            pltpu.VMEM((tile, 2 * HS), f32),
        ],
        compiler_params=pltpu.CompilerParams(vmem_limit_bytes=40 * 2**20),
        name="attend",
    )(request_length, qbuf, kbuf, vbuf)

    half = rows // 2
    chunks = 2 * width // COLS
    parts = len(PARTS)
    return pl.pallas_call(
        project_kernel,
        out_shape=jax.ShapeDtypeStruct((rows, 2 * width), bf16),
        in_specs=[SMEM, SMEM] + [ANY] * 6,
        out_specs=ANY,
        scratch_shapes=[
            pltpu.VMEM((2, half, width), bf16),
            pltpu.VMEM((width, 2 * width), bf16),
            pltpu.VMEM((width, 2 * width), bf16),
            pltpu.VMEM((rank, width), bf16),
            pltpu.VMEM((rank, 2 * width), bf16),
            pltpu.VMEM((half, 2 * width), bf16),
            pltpu.VMEM((half, 2 * width), bf16),
            pltpu.VMEM((half, width), bf16),
            pltpu.VMEM((half, rank), f32),
            pltpu.VMEM((half, rank), f32),
            pltpu.VMEM((half, 2 * width), f32),
            pltpu.VMEM((chunks, half, COLS), bf16),
            pltpu.VMEM((chunks, half, COLS), bf16),
            pltpu.VMEM((half, rank), bf16),
            pltpu.VMEM((half, rank), bf16),
            pltpu.VMEM((half, 2 * width), bf16),
            dma((6,)), dma((parts, 2, steps)), dma((parts,)),
            dma((parts, chunks, 2)), dma((parts, 2)), dma((parts, chunks, 3)),
        ],
        compiler_params=pltpu.CompilerParams(
            has_side_effects=True, collective_id=2, vmem_limit_bytes=48 * 2**20
        ),
        name="project",
    )(request_length, request_adapters, o, hidden, hbuf, output_weight, down, up)


def solution(mesh):
    return jax.shard_map(
        local,
        mesh=mesh,
        in_specs=(
            P("cfg", "seq", "head"),
            P("cfg", "seq", "head"),
            P("cfg", "seq", "head"),
            P("cfg", "seq", "head"),
            P("head", None),
            P(None, "head", None),
            P(None, None, "head"),
            P(),
            P(),
        ),
        out_specs=P("seq", "head"),
        check_vma=False,
    )
```

```python
import functools
import math

import jax
import jax.numpy as jnp
from jax import lax
from jax.experimental import pallas as pl
from jax.experimental.pallas import tpu as pltpu
from jax.sharding import PartitionSpec as P

MESH = pl.DeviceIdType.MESH
HS = 128
GUIDE = 5.0
BK = 1536
PAIR = 2
PARTS = ((0, 64), (64, 48))
COLS = 512
ANY = pl.BlockSpec(memory_space=pl.ANY)
SMEM = pl.BlockSpec(memory_space=pltpu.SMEM)
VMEM = pl.BlockSpec(memory_space=pltpu.VMEM)


def place(head, branch):
    y = head // 2
    x = 2 * (head % 2) + (y + branch) % 2
    p = jnp.where(head < 8, y * 4 + x, jnp.where(head == 8, 1 - branch, 11 - branch))
    return (p // 4) * 8 + branch * 4 + p % 4


def role(s):
    x, y, branch = s % 4, s // 8, (s // 4) % 2
    p = y * 4 + x
    board = (x + y) % 2 == branch
    late = jnp.where(p == 1 - branch, 8, 9)
    active = jnp.logical_or(board, jnp.logical_or(p == 1 - branch, p == 11 - branch))
    return active, jnp.where(board, y * 2 + x // 2, late), branch


def signal(semaphore, *device):
    pl.semaphore_signal(semaphore, inc=1, device_id=device, device_id_type=MESH)


def scatter_kernel(
    q_ref, k_ref, v_ref, hid_ref, kbuf, vbuf, qbuf, hbuf,
    send_sem, kv_sem, q_sem, hid_sem, fwd_sem,
):
    b = lax.axis_index("cfg")
    s = lax.axis_index("seq")
    g = lax.axis_index("head")
    rows = q_ref.shape[1]
    heads = q_ref.shape[2] // HS
    half = hbuf.shape[0]
    active, _, branch = role(s)
    seqs = 32

    barrier = pltpu.get_barrier_semaphore()
    signal(barrier, 1 - b, s, g)

    @pl.when(active)
    def _():
        @pl.loop(0, seqs)
        def _(i):
            t = (s + i) % seqs

            @pl.when(jnp.logical_not(jnp.logical_and(t == s, branch == b)))
            def _():
                signal(barrier, branch, t, g)

    own = jnp.where(jnp.logical_and(active, branch == b), 1, 0)
    pl.semaphore_wait(barrier, 2 * heads + 1 - own)

    groups = kv_sem.shape[0]
    per = kbuf.shape[0] // groups

    other = pltpu.make_async_remote_copy(
        src_ref=hid_ref.at[0, pl.ds(pl.multiple_of((1 - b) * half, 16), half), :],
        dst_ref=hbuf,
        send_sem=hid_sem.at[0],
        recv_sem=hid_sem.at[1],
        device_id=(1 - b, s, g),
        device_id_type=MESH,
    )

    row0 = pl.multiple_of(s * rows, 32)
    qrow0 = pl.multiple_of((s // 2) * rows, 32)
    kind = (
        (k_ref, lambda: kbuf.at[pl.ds(row0, rows), :], kv_sem.at[s // (32 // groups)], 0),
        (v_ref, lambda: vbuf.at[pl.ds(row0, rows), :], kv_sem.at[s // (32 // groups)], 1),
        (q_ref, lambda: qbuf.at[pl.ds(qrow0, rows), :], q_sem, s % 2),
    )

    def each(i, act, kinds=(0, 1, 2)):
        h = (i + s) % heads
        target = place(h, b)
        for n in kinds:
            src, dst, sem, core = kind[n]
            piece = src.at[0, :, pl.ds(pl.multiple_of(h * HS, HS), HS)]
            mine = jnp.logical_and(target == s, core == b)
            act(n, piece, dst(), sem, core, target, mine, i)

    def start(n, piece, dst, sem, core, target, mine, i):
        @pl.when(mine)
        def _():
            pltpu.make_async_copy(piece, dst, sem).start()

        @pl.when(jnp.logical_not(mine))
        def _():
            pltpu.make_async_remote_copy(
                src_ref=piece, dst_ref=dst, send_sem=send_sem.at[i * 3 + n], recv_sem=sem,
                device_id=(core, target, g), device_id_type=MESH,
            ).start()

    def finish(n, piece, dst, sem, core, target, mine, i):
        @pl.when(jnp.logical_not(mine))
        def _():
            pltpu.make_async_remote_copy(
                src_ref=piece, dst_ref=dst, send_sem=send_sem.at[i * 3 + n], recv_sem=sem,
                device_id=(core, target, g), device_id_type=MESH,
            ).wait_send()

    for n in range(3):

        @pl.loop(0, heads)
        def _(i):
            each(i, start, (n,))

    other.start()

    def forward(buf, n):
        part = buf.at[pl.ds(n * per, per), :]
        return pltpu.make_async_remote_copy(
            src_ref=part, dst_ref=part, send_sem=fwd_sem.at[0, n], recv_sem=fwd_sem.at[1, n],
            device_id=(1 - b, s, g), device_id_type=MESH,
        )

    def landed(buf, sem):
        pltpu.make_async_copy(buf, buf, sem).wait()

    for core, (got, came) in enumerate(((kbuf, vbuf), (vbuf, kbuf))):

        @pl.when(jnp.logical_and(active, b == core))
        def _():
            for n in range(groups):
                landed(got.at[pl.ds(n * per, per), :], kv_sem.at[n])
                forward(got, n).start()
            for n in range(groups):
                forward(got, n).wait_send()
                forward(came, n).wait_recv()
            landed(qbuf, q_sem)

    @pl.loop(0, heads)
    def _(i):
        each(i, finish)

    other.wait()


def attention_kernel(
    len_ref, q_ref, k_ref, v_ref, w_ref, o_ref, kept_ref, s_ref, m_ref, acc_ref, w_sem
):
    c = lax.axis_index("cfg")
    s = lax.axis_index("seq")
    active, _, _ = role(s)
    rows = acc_ref.shape[0]
    piece = rows // PAIR
    tokens = k_ref.shape[0]
    factor = math.log2(math.e) / math.sqrt(HS)
    fetch = pltpu.make_async_copy(w_ref, kept_ref, w_sem)
    fetch.start()
    e0 = len_ref[0]
    e1 = e0 + len_ref[1]
    e2 = e1 + len_ref[2]

    def segment(pos):
        return (
            (pos >= e0).astype(jnp.int32)
            + (pos >= e1).astype(jnp.int32)
            + (pos >= e2).astype(jnp.int32)
        )

    @pl.loop(0, jnp.where(active, q_ref.shape[0] // rows, 0))
    def _(tile):
        first = (2 * PAIR * tile + c) * piece
        last = first + (2 * PAIR - 1) * piece - 1
        own = pl.ds(pl.multiple_of(tile * rows, 32), rows)
        seg_first = segment(first)
        seg_last = segment(last)
        starts = (0, e0, e1, e2)
        ends = (e0, e1, e2, tokens)
        lo = jnp.int32(0)
        hi = jnp.int32(tokens)
        for n in range(4):
            lo = jnp.where(seg_first == n, starts[n], lo)
            hi = jnp.where(seg_last == n, ends[n], hi)
        base = (lo // 32) * 32
        blocks = pl.cdiv(hi - base, BK)
        single = seg_first == seg_last
        row = lax.broadcasted_iota(jnp.int32, (rows, 1), 0)
        seg_q = segment(first + row + (row // piece) * piece)
        m_ref[...] = jnp.full_like(m_ref, -1e30)

        def widest(x):
            out = m_ref[...]
            for n in range(BK // HS):
                out = jnp.maximum(out, x[:, n * HS : (n + 1) * HS])
            m_ref[...] = out

        def scores(at):
            return lax.dot_general(
                q_ref[own, :], k_ref[pl.ds(at, BK), :], (((1,), (1,)), ((), ())),
                preferred_element_type=jnp.float32,
            )

        @pl.loop(0, blocks)
        def _(n):
            logical = base + n * BK
            at = pl.multiple_of(jnp.minimum(logical, tokens - BK), 32)
            whole = jnp.logical_and(
                single, jnp.logical_and(logical >= lo, logical + BK <= hi)
            )

            @pl.when(whole)
            def _():
                score = scores(at)
                s_ref[n] = score
                widest(score)

            @pl.when(jnp.logical_not(whole))
            def _():
                pos = at + lax.broadcasted_iota(jnp.int32, (1, BK), 1)
                seg_k = jnp.where(pos >= logical, segment(pos), -1)
                score = jnp.where(seg_q == seg_k, scores(at), -jnp.inf)
                s_ref[n] = score
                widest(score)

        m_ref[...] = jnp.broadcast_to(
            jnp.max(m_ref[...], axis=1, keepdims=True), m_ref.shape
        )
        acc_ref[...] = jnp.zeros_like(acc_ref)

        @pl.loop(0, blocks)
        def _(n):
            at = pl.multiple_of(jnp.minimum(base + n * BK, tokens - BK), 32)
            top = m_ref[...]
            weight = jnp.concatenate(
                [
                    jnp.exp2((s_ref[n, :, j * HS : (j + 1) * HS] - top) * factor).astype(
                        jnp.bfloat16
                    )
                    for j in range(BK // HS)
                ],
                axis=1,
            )
            values = jnp.concatenate(
                [v_ref[pl.ds(at, BK), :], jnp.ones((BK, HS), jnp.bfloat16)], axis=1
            )
            acc_ref[...] += jnp.dot(weight, values, preferred_element_type=jnp.float32)

        o_ref[own, :] = (acc_ref[:, :HS] / acc_ref[:, HS:]).astype(o_ref.dtype)

    fetch.wait()


def project_kernel(
    len_ref, ad_ref, o_ref, hid_ref, hbuf, w_ref, down_ref, up_ref, out_ref,
    att, dv, inner, picked, pm, psend, precv, isend, irecv, outv,
    o_send, o_sem, p_sem, i_sem, out_sem,
):
    b = lax.axis_index("cfg")
    s = lax.axis_index("seq")
    g = lax.axis_index("head")
    active, head, branch = role(s)
    half, width = outv.shape
    rows = 2 * half
    heads = att.shape[2] // HS
    blocks = o_ref.shape[0] // rows
    chunks = range(width // COLS)
    top = pl.multiple_of(b * half, 16)

    barrier = pltpu.get_barrier_semaphore()
    signal(barrier, 1 - b, s, g)
    signal(barrier, b, s, 1 - g)

    for origin in range(2):

        @pl.loop(0, heads)
        def _(i):
            t = place((i + s) % heads, origin)

            @pl.when(jnp.logical_not(jnp.logical_and(t == s, s % 2 == b)))
            def _():
                signal(barrier, s % 2, t, g)

    own = jnp.where(s % 2 == b, 1, 0)
    pl.semaphore_wait(barrier, 2 + jnp.where(active, 2 * blocks - own, 0))

    def send_o(i, n, core, go):
        j = 2 * i + b
        first, count = PARTS[n]
        piece = o_ref.at[pl.ds(pl.multiple_of(i * rows + core * half + first, 16), count), :]
        dst = att.at[branch, pl.ds(first, count), pl.ds(pl.multiple_of(head * HS, HS), HS)]
        here = jnp.logical_and(j == s, core == b)

        @pl.when(here)
        def _():
            if go:
                pltpu.make_async_copy(piece, dst, o_sem.at[n]).start()

        @pl.when(jnp.logical_not(here))
        def _():
            copy = pltpu.make_async_remote_copy(
                src_ref=piece, dst_ref=dst, send_sem=o_send.at[n, core, i], recv_sem=o_sem.at[n],
                device_id=(core, j, g), device_id_type=MESH,
            )
            if go:
                copy.start()
            else:
                copy.wait_send()

    @pl.when(active)
    def _():
        for n in range(len(PARTS)):

            @pl.loop(0, blocks)
            def _(i):
                for core in range(2):
                    send_o((i + s // 2) % blocks, n, core, True)

    def partner(src, dst, sems):
        return pltpu.make_async_remote_copy(
            src_ref=src, dst_ref=dst, send_sem=sems.at[0], recv_sem=sems.at[1],
            device_id=(b, s, 1 - g), device_id_type=MESH,
        )

    rank = down_ref.shape[0] // 8
    pos = s * rows + b * half + lax.broadcasted_iota(jnp.int32, picked.shape, 0)
    lane = lax.broadcasted_iota(jnp.int32, picked.shape, 1)
    e0 = len_ref[0]
    e1 = e0 + len_ref[1]
    e2 = e1 + len_ref[2]
    adapter = jnp.where(
        pos < e1,
        jnp.where(pos < e0, ad_ref[0], ad_ref[1]),
        jnp.where(pos < e2, ad_ref[2], ad_ref[3]),
    )
    picked[...] = ((lane // rank) == adapter).astype(jnp.float32)
    scale_m = jnp.where(b == 0, GUIDE, 1.0 - GUIDE).astype(jnp.float32)
    scale_o = jnp.where(b == 0, 1.0 - GUIDE, GUIDE).astype(jnp.float32)
    hm = hid_ref[0, pl.ds(top, half), :].astype(jnp.float32)
    pm[...] = scale_m * hm + scale_o * hbuf[...].astype(jnp.float32)

    def column(c):
        return slice(c * COLS, (c + 1) * COLS)

    def weight(side, c):
        return w_ref[:, pl.ds(pl.multiple_of(side * width + c * COLS, COLS), COLS)]

    for n, (first, count) in enumerate(PARTS):
        sl = slice(first, first + count)
        came = att.at[:, pl.ds(first, count), :]
        pltpu.make_async_copy(came, came, o_sem.at[n]).wait()
        dv[sl, :] = (
            GUIDE * att[0, sl, :].astype(jnp.float32)
            + (1.0 - GUIDE) * att[1, sl, :].astype(jnp.float32)
        ).astype(jnp.bfloat16)
        for c in chunks:
            psend[c, sl, :] = jnp.dot(
                dv[sl, :], weight(1 - g, c), preferred_element_type=jnp.float32
            ).astype(jnp.bfloat16)
            partner(psend.at[c, sl, :], precv.at[c, sl, :], p_sem.at[n, c]).start()
            if c == 0:
                inner[sl, :] = (
                    lax.dot_general(
                        dv[sl, :], down_ref[...], (((1,), (1,)), ((), ())),
                        preferred_element_type=jnp.float32,
                    )
                    * picked[sl, :]
                )
                isend[sl, :] = inner[sl, :].astype(jnp.bfloat16)
                partner(isend.at[sl, :], irecv.at[sl, :], i_sem.at[n]).start()
    for c in chunks:
        pm[:, column(c)] += jnp.dot(
            dv[...], weight(g, c), preferred_element_type=jnp.float32
        )
    for n, (first, count) in enumerate(PARTS):
        sl = slice(first, first + count)
        partner(isend.at[sl, :], irecv.at[sl, :], i_sem.at[n]).wait()
    both = (inner[...] + irecv[...].astype(jnp.float32)).astype(jnp.bfloat16)
    for c in chunks:
        pm[:, column(c)] += jnp.dot(both, up_ref[:, column(c)], preferred_element_type=jnp.float32)
    last = []
    for n, (first, count) in enumerate(PARTS):
        sl = slice(first, first + count)
        for c in chunks:
            partner(psend.at[c, sl, :], precv.at[c, sl, :], p_sem.at[n, c]).wait()
            outv[sl, column(c)] = (
                pm[sl, column(c)] + precv[c, sl, :].astype(jnp.float32)
            ).astype(jnp.bfloat16)
            piece = outv.at[sl, pl.ds(c * COLS, COLS)]
            result = out_ref.at[pl.ds(pl.multiple_of(top + first, 16), count), pl.ds(c * COLS, COLS)]
            last.append(
                pltpu.make_async_remote_copy(
                    src_ref=piece, dst_ref=result,
                    send_sem=out_sem.at[n, c, 0], recv_sem=out_sem.at[n, c, 1],
                    device_id=(1 - b, s, g), device_id_type=MESH,
                )
            )
            last.append(pltpu.make_async_copy(piece, result, out_sem.at[n, c, 2]))
            last[-2].start()
            last[-1].start()

    @pl.when(active)
    def _():
        for n in range(len(PARTS)):

            @pl.loop(0, blocks)
            def _(i):
                for core in range(2):
                    send_o(i, n, core, False)

    for copy in last:
        copy.wait()


def local(
    hidden, queries, keys, values, output_weight, adapter_down_weight, adapter_up_weight,
    request_adapters, request_length,
):
    rows, width = queries.shape[1:]
    tokens = rows * 32
    bf16, f32 = jnp.bfloat16, jnp.float32
    dma = pltpu.SemaphoreType.DMA
    down = adapter_down_weight.transpose(0, 2, 1).reshape(-1, width)
    up = adapter_up_weight.reshape(-1, adapter_up_weight.shape[2])
    rank = up.shape[0]

    kbuf, vbuf, qbuf, hbuf = pl.pallas_call(
        scatter_kernel,
        out_shape=(
            jax.ShapeDtypeStruct((tokens, HS), bf16),
            jax.ShapeDtypeStruct((tokens, HS), bf16),
            jax.ShapeDtypeStruct((tokens // 2, HS), bf16),
            jax.ShapeDtypeStruct((rows // 2, 2 * width), bf16),
        ),
        in_specs=[ANY] * 4,
        out_specs=(ANY,) * 4,
        scratch_shapes=[dma((30,)), dma((4,)), dma, dma((2,)), dma((2, 4))],
        compiler_params=pltpu.CompilerParams(
            has_side_effects=True, collective_id=1, vmem_limit_bytes=2**20
        ),
        name="scatter_heads",
    )(*(pltpu.with_memory_space_constraint(x, pltpu.HBM) for x in (queries, keys, values, hidden)))

    steps = tokens // 2 // rows
    tile = PAIR * rows
    o, kept = pl.pallas_call(
        attention_kernel,
        out_shape=(
            jax.ShapeDtypeStruct((tokens // 2, HS), bf16),
            jax.ShapeDtypeStruct(output_weight.shape, bf16),
        ),
        in_specs=[SMEM, VMEM, VMEM, VMEM, ANY],
        out_specs=(VMEM, ANY),
        scratch_shapes=[
            pltpu.VMEM((pl.cdiv(tokens, BK), tile, BK), f32),
            pltpu.VMEM((tile, HS), f32),
            pltpu.VMEM((tile, 2 * HS), f32),
            dma,
        ],
        compiler_params=pltpu.CompilerParams(vmem_limit_bytes=24 * 2**20),
        name="attend",
    )(request_length, qbuf, kbuf, vbuf, pltpu.with_memory_space_constraint(output_weight, pltpu.HBM))

    half = rows // 2
    chunks = 2 * width // COLS
    parts = len(PARTS)
    return pl.pallas_call(
        project_kernel,
        out_shape=jax.ShapeDtypeStruct((rows, 2 * width), bf16),
        in_specs=[SMEM, SMEM, ANY] + [VMEM] * 5,
        out_specs=ANY,
        scratch_shapes=[
            pltpu.VMEM((2, half, width), bf16),
            pltpu.VMEM((half, width), bf16),
            pltpu.VMEM((half, rank), f32),
            pltpu.VMEM((half, rank), f32),
            pltpu.VMEM((half, 2 * width), f32),
            pltpu.VMEM((chunks, half, COLS), bf16),
            pltpu.VMEM((chunks, half, COLS), bf16),
            pltpu.VMEM((half, rank), bf16),
            pltpu.VMEM((half, rank), bf16),
            pltpu.VMEM((half, 2 * width), bf16),
            dma((parts, 2, steps)), dma((parts,)),
            dma((parts, chunks, 2)), dma((parts, 2)), dma((parts, chunks, 3)),
        ],
        compiler_params=pltpu.CompilerParams(
            has_side_effects=True, collective_id=2, vmem_limit_bytes=16 * 2**20
        ),
        name="project",
    )(request_length, request_adapters, o, hidden, hbuf, kept, down, up)


def solution(mesh):
    return jax.shard_map(
        local,
        mesh=mesh,
        in_specs=(
            P("cfg", "seq", "head"),
            P("cfg", "seq", "head"),
            P("cfg", "seq", "head"),
            P("cfg", "seq", "head"),
            P("head", None),
            P(None, "head", None),
            P(None, None, "head"),
            P(),
            P(),
        ),
        out_specs=P("seq", "head"),
        check_vma=False,
    )
```

```python
import functools
import math

import jax
import jax.numpy as jnp
from jax import lax
from jax.experimental import pallas as pl
from jax.experimental.pallas import tpu as pltpu
from jax.sharding import PartitionSpec as P

MESH = pl.DeviceIdType.MESH
HS = 128
GUIDE = 5.0
BK = 1536
PAIR = 2
PARTS = ((0, 32), (32, 80))
COLS = 512
ANY = pl.BlockSpec(memory_space=pl.ANY)
SMEM = pl.BlockSpec(memory_space=pltpu.SMEM)
VMEM = pl.BlockSpec(memory_space=pltpu.VMEM)


def place(head, branch):
    y = head // 2
    x = 2 * (head % 2) + (y + branch) % 2
    p = jnp.where(head < 8, y * 4 + x, jnp.where(head == 8, 1 - branch, 11 - branch))
    return (p // 4) * 8 + branch * 4 + p % 4


def role(s):
    x, y, branch = s % 4, s // 8, (s // 4) % 2
    p = y * 4 + x
    board = (x + y) % 2 == branch
    late = jnp.where(p == 1 - branch, 8, 9)
    active = jnp.logical_or(board, jnp.logical_or(p == 1 - branch, p == 11 - branch))
    return active, jnp.where(board, y * 2 + x // 2, late), branch


def signal(semaphore, *device):
    pl.semaphore_signal(semaphore, inc=1, device_id=device, device_id_type=MESH)


def scatter_kernel(
    q_ref, k_ref, v_ref, hid_ref, kbuf, vbuf, qbuf, hbuf,
    send_sem, kv_sem, q_sem, hid_sem, fwd_sem,
):
    b = lax.axis_index("cfg")
    s = lax.axis_index("seq")
    g = lax.axis_index("head")
    rows = q_ref.shape[1]
    heads = q_ref.shape[2] // HS
    half = hbuf.shape[0]
    active, _, branch = role(s)
    seqs = 32

    barrier = pltpu.get_barrier_semaphore()
    signal(barrier, 1 - b, s, g)

    @pl.when(active)
    def _():
        @pl.loop(0, seqs)
        def _(i):
            t = (s + i) % seqs

            @pl.when(jnp.logical_not(jnp.logical_and(t == s, branch == b)))
            def _():
                signal(barrier, branch, t, g)

    own = jnp.where(jnp.logical_and(active, branch == b), 1, 0)
    pl.semaphore_wait(barrier, 2 * heads + 1 - own)

    groups = kv_sem.shape[0]
    per = kbuf.shape[0] // groups

    other = pltpu.make_async_remote_copy(
        src_ref=hid_ref.at[0, pl.ds(pl.multiple_of((1 - b) * half, 16), half), :],
        dst_ref=hbuf,
        send_sem=hid_sem.at[0],
        recv_sem=hid_sem.at[1],
        device_id=(1 - b, s, g),
        device_id_type=MESH,
    )

    row0 = pl.multiple_of(s * rows, 32)
    qrow0 = pl.multiple_of((s // 2) * rows, 32)
    kind = (
        (k_ref, lambda: kbuf.at[pl.ds(row0, rows), :], kv_sem.at[s // (32 // groups)], 0),
        (v_ref, lambda: vbuf.at[pl.ds(row0, rows), :], kv_sem.at[s // (32 // groups)], 1),
        (q_ref, lambda: qbuf.at[pl.ds(qrow0, rows), :], q_sem, s % 2),
    )

    def each(i, act, kinds=(0, 1, 2)):
        h = (i + s) % heads
        target = place(h, b)
        for n in kinds:
            src, dst, sem, core = kind[n]
            piece = src.at[0, :, pl.ds(pl.multiple_of(h * HS, HS), HS)]
            mine = jnp.logical_and(target == s, core == b)
            act(n, piece, dst(), sem, core, target, mine, i)

    def start(n, piece, dst, sem, core, target, mine, i):
        @pl.when(mine)
        def _():
            pltpu.make_async_copy(piece, dst, sem).start()

        @pl.when(jnp.logical_not(mine))
        def _():
            pltpu.make_async_remote_copy(
                src_ref=piece, dst_ref=dst, send_sem=send_sem.at[i * 3 + n], recv_sem=sem,
                device_id=(core, target, g), device_id_type=MESH,
            ).start()

    def finish(n, piece, dst, sem, core, target, mine, i):
        @pl.when(jnp.logical_not(mine))
        def _():
            pltpu.make_async_remote_copy(
                src_ref=piece, dst_ref=dst, send_sem=send_sem.at[i * 3 + n], recv_sem=sem,
                device_id=(core, target, g), device_id_type=MESH,
            ).wait_send()

    for n in range(3):

        @pl.loop(0, heads)
        def _(i):
            each(i, start, (n,))

    other.start()

    def forward(buf, n):
        part = buf.at[pl.ds(n * per, per), :]
        return pltpu.make_async_remote_copy(
            src_ref=part, dst_ref=part, send_sem=fwd_sem.at[0, n], recv_sem=fwd_sem.at[1, n],
            device_id=(1 - b, s, g), device_id_type=MESH,
        )

    def landed(buf, sem):
        pltpu.make_async_copy(buf, buf, sem).wait()

    for core, (got, came) in enumerate(((kbuf, vbuf), (vbuf, kbuf))):

        @pl.when(jnp.logical_and(active, b == core))
        def _():
            for n in range(groups):
                landed(got.at[pl.ds(n * per, per), :], kv_sem.at[n])
                forward(got, n).start()
            for n in range(groups):
                forward(got, n).wait_send()
                forward(came, n).wait_recv()
            landed(qbuf, q_sem)

    @pl.loop(0, heads)
    def _(i):
        each(i, finish)

    other.wait()


def attention_kernel(
    len_ref, q_ref, k_ref, v_ref, w_ref, o_ref, kept_ref, s_ref, m_ref, acc_ref, w_sem
):
    c = lax.axis_index("cfg")
    s = lax.axis_index("seq")
    active, _, _ = role(s)
    rows = acc_ref.shape[0]
    piece = rows // PAIR
    tokens = k_ref.shape[0]
    factor = math.log2(math.e) / math.sqrt(HS)
    fetch = pltpu.make_async_copy(w_ref, kept_ref, w_sem)
    fetch.start()
    e0 = len_ref[0]
    e1 = e0 + len_ref[1]
    e2 = e1 + len_ref[2]

    def segment(pos):
        return (
            (pos >= e0).astype(jnp.int32)
            + (pos >= e1).astype(jnp.int32)
            + (pos >= e2).astype(jnp.int32)
        )

    @pl.loop(0, jnp.where(active, q_ref.shape[0] // rows, 0))
    def _(tile):
        first = (2 * PAIR * tile + c) * piece
        last = first + (2 * PAIR - 1) * piece - 1
        own = pl.ds(pl.multiple_of(tile * rows, 32), rows)
        seg_first = segment(first)
        seg_last = segment(last)
        starts = (0, e0, e1, e2)
        ends = (e0, e1, e2, tokens)
        lo = jnp.int32(0)
        hi = jnp.int32(tokens)
        for n in range(4):
            lo = jnp.where(seg_first == n, starts[n], lo)
            hi = jnp.where(seg_last == n, ends[n], hi)
        base = (lo // 32) * 32
        blocks = pl.cdiv(hi - base, BK)
        single = seg_first == seg_last
        row = lax.broadcasted_iota(jnp.int32, (rows, 1), 0)
        seg_q = segment(first + row + (row // piece) * piece)
        m_ref[...] = jnp.full_like(m_ref, -1e30)

        def widest(x):
            out = m_ref[...]
            for n in range(BK // HS):
                out = jnp.maximum(out, x[:, n * HS : (n + 1) * HS])
            m_ref[...] = out

        def scores(at):
            return lax.dot_general(
                q_ref[own, :], k_ref[pl.ds(at, BK), :], (((1,), (1,)), ((), ())),
                preferred_element_type=jnp.float32,
            )

        @pl.loop(0, blocks)
        def _(n):
            logical = base + n * BK
            at = pl.multiple_of(jnp.minimum(logical, tokens - BK), 32)
            whole = jnp.logical_and(
                single, jnp.logical_and(logical >= lo, logical + BK <= hi)
            )

            @pl.when(whole)
            def _():
                score = scores(at)
                s_ref[n] = score
                widest(score)

            @pl.when(jnp.logical_not(whole))
            def _():
                pos = at + lax.broadcasted_iota(jnp.int32, (1, BK), 1)
                seg_k = jnp.where(pos >= logical, segment(pos), -1)
                score = jnp.where(seg_q == seg_k, scores(at), -jnp.inf)
                s_ref[n] = score
                widest(score)

        m_ref[...] = jnp.broadcast_to(
            jnp.max(m_ref[...], axis=1, keepdims=True), m_ref.shape
        )
        acc_ref[...] = jnp.zeros_like(acc_ref)

        @pl.loop(0, blocks)
        def _(n):
            at = pl.multiple_of(jnp.minimum(base + n * BK, tokens - BK), 32)
            top = m_ref[...]
            weight = jnp.concatenate(
                [
                    jnp.exp2((s_ref[n, :, j * HS : (j + 1) * HS] - top) * factor).astype(
                        jnp.bfloat16
                    )
                    for j in range(BK // HS)
                ],
                axis=1,
            )
            values = jnp.concatenate(
                [v_ref[pl.ds(at, BK), :], jnp.ones((BK, HS), jnp.bfloat16)], axis=1
            )
            acc_ref[...] += jnp.dot(weight, values, preferred_element_type=jnp.float32)

        o_ref[own, :] = (acc_ref[:, :HS] / acc_ref[:, HS:]).astype(o_ref.dtype)

    fetch.wait()


def project_kernel(
    len_ref, ad_ref, o_ref, hid_ref, hbuf, w_ref, down_ref, up_ref, out_ref,
    att, dv, inner, picked, pm, psend, precv, isend, irecv, outv,
    o_send, o_sem, p_sem, i_sem, out_sem,
):
    b = lax.axis_index("cfg")
    s = lax.axis_index("seq")
    g = lax.axis_index("head")
    active, head, branch = role(s)
    half, width = outv.shape
    rows = 2 * half
    heads = att.shape[2] // HS
    blocks = o_ref.shape[0] // rows
    chunks = range(width // COLS)
    top = pl.multiple_of(b * half, 16)

    barrier = pltpu.get_barrier_semaphore()
    signal(barrier, 1 - b, s, g)
    signal(barrier, b, s, 1 - g)

    for origin in range(2):

        @pl.loop(0, heads)
        def _(i):
            t = place((i + s) % heads, origin)

            @pl.when(jnp.logical_not(jnp.logical_and(t == s, s % 2 == b)))
            def _():
                signal(barrier, s % 2, t, g)

    own = jnp.where(s % 2 == b, 1, 0)
    pl.semaphore_wait(barrier, 2 + jnp.where(active, 2 * blocks - own, 0))

    def send_o(i, n, core, go):
        j = 2 * i + b
        first, count = PARTS[n]
        piece = o_ref.at[pl.ds(pl.multiple_of(i * rows + core * half + first, 16), count), :]
        dst = att.at[branch, pl.ds(first, count), pl.ds(pl.multiple_of(head * HS, HS), HS)]
        here = jnp.logical_and(j == s, core == b)

        @pl.when(here)
        def _():
            if go:
                pltpu.make_async_copy(piece, dst, o_sem.at[n]).start()

        @pl.when(jnp.logical_not(here))
        def _():
            copy = pltpu.make_async_remote_copy(
                src_ref=piece, dst_ref=dst, send_sem=o_send.at[n, core, i], recv_sem=o_sem.at[n],
                device_id=(core, j, g), device_id_type=MESH,
            )
            if go:
                copy.start()
            else:
                copy.wait_send()

    @pl.when(active)
    def _():
        for n in range(len(PARTS)):

            @pl.loop(0, blocks)
            def _(i):
                for core in range(2):
                    send_o((i + s // 2) % blocks, n, core, True)

    def partner(src, dst, sems):
        return pltpu.make_async_remote_copy(
            src_ref=src, dst_ref=dst, send_sem=sems.at[0], recv_sem=sems.at[1],
            device_id=(b, s, 1 - g), device_id_type=MESH,
        )

    rank = down_ref.shape[0] // 8
    pos = s * rows + b * half + lax.broadcasted_iota(jnp.int32, picked.shape, 0)
    lane = lax.broadcasted_iota(jnp.int32, picked.shape, 1)
    e0 = len_ref[0]
    e1 = e0 + len_ref[1]
    e2 = e1 + len_ref[2]
    adapter = jnp.where(
        pos < e1,
        jnp.where(pos < e0, ad_ref[0], ad_ref[1]),
        jnp.where(pos < e2, ad_ref[2], ad_ref[3]),
    )
    picked[...] = ((lane // rank) == adapter).astype(jnp.float32)
    scale_m = jnp.where(b == 0, GUIDE, 1.0 - GUIDE).astype(jnp.float32)
    scale_o = jnp.where(b == 0, 1.0 - GUIDE, GUIDE).astype(jnp.float32)
    hm = hid_ref[0, pl.ds(top, half), :].astype(jnp.float32)
    pm[...] = scale_m * hm + scale_o * hbuf[...].astype(jnp.float32)

    def column(c):
        return slice(c * COLS, (c + 1) * COLS)

    def weight(side, c):
        return w_ref[:, pl.ds(pl.multiple_of(side * width + c * COLS, COLS), COLS)]

    for n, (first, count) in enumerate(PARTS):
        sl = slice(first, first + count)
        came = att.at[:, pl.ds(first, count), :]
        pltpu.make_async_copy(came, came, o_sem.at[n]).wait()
        dv[sl, :] = (
            GUIDE * att[0, sl, :].astype(jnp.float32)
            + (1.0 - GUIDE) * att[1, sl, :].astype(jnp.float32)
        ).astype(jnp.bfloat16)
        for c in chunks:
            psend[c, sl, :] = jnp.dot(
                dv[sl, :], weight(1 - g, c), preferred_element_type=jnp.float32
            ).astype(jnp.bfloat16)
            partner(psend.at[c, sl, :], precv.at[c, sl, :], p_sem.at[n, c]).start()
            if c == 0:
                inner[sl, :] = (
                    lax.dot_general(
                        dv[sl, :], down_ref[...], (((1,), (1,)), ((), ())),
                        preferred_element_type=jnp.float32,
                    )
                    * picked[sl, :]
                )
                isend[sl, :] = inner[sl, :].astype(jnp.bfloat16)
                partner(isend.at[sl, :], irecv.at[sl, :], i_sem.at[n]).start()
    for c in chunks:
        pm[:, column(c)] += jnp.dot(
            dv[...], weight(g, c), preferred_element_type=jnp.float32
        )
    for n, (first, count) in enumerate(PARTS):
        sl = slice(first, first + count)
        partner(isend.at[sl, :], irecv.at[sl, :], i_sem.at[n]).wait()
    both = (inner[...] + irecv[...].astype(jnp.float32)).astype(jnp.bfloat16)
    for c in chunks:
        pm[:, column(c)] += jnp.dot(both, up_ref[:, column(c)], preferred_element_type=jnp.float32)
    last = []
    for n, (first, count) in enumerate(PARTS):
        sl = slice(first, first + count)
        for c in chunks:
            partner(psend.at[c, sl, :], precv.at[c, sl, :], p_sem.at[n, c]).wait()
            outv[sl, column(c)] = (
                pm[sl, column(c)] + precv[c, sl, :].astype(jnp.float32)
            ).astype(jnp.bfloat16)
            piece = outv.at[sl, pl.ds(c * COLS, COLS)]
            result = out_ref.at[pl.ds(pl.multiple_of(top + first, 16), count), pl.ds(c * COLS, COLS)]
            last.append(
                pltpu.make_async_remote_copy(
                    src_ref=piece, dst_ref=result,
                    send_sem=out_sem.at[n, c, 0], recv_sem=out_sem.at[n, c, 1],
                    device_id=(1 - b, s, g), device_id_type=MESH,
                )
            )
            last.append(pltpu.make_async_copy(piece, result, out_sem.at[n, c, 2]))
            last[-2].start()
            last[-1].start()

    @pl.when(active)
    def _():
        for n in range(len(PARTS)):

            @pl.loop(0, blocks)
            def _(i):
                for core in range(2):
                    send_o(i, n, core, False)

    for copy in last:
        copy.wait()


def local(
    hidden, queries, keys, values, output_weight, adapter_down_weight, adapter_up_weight,
    request_adapters, request_length,
):
    rows, width = queries.shape[1:]
    tokens = rows * 32
    bf16, f32 = jnp.bfloat16, jnp.float32
    dma = pltpu.SemaphoreType.DMA
    down = adapter_down_weight.transpose(0, 2, 1).reshape(-1, width)
    up = adapter_up_weight.reshape(-1, adapter_up_weight.shape[2])
    rank = up.shape[0]

    kbuf, vbuf, qbuf, hbuf = pl.pallas_call(
        scatter_kernel,
        out_shape=(
            jax.ShapeDtypeStruct((tokens, HS), bf16),
            jax.ShapeDtypeStruct((tokens, HS), bf16),
            jax.ShapeDtypeStruct((tokens // 2, HS), bf16),
            jax.ShapeDtypeStruct((rows // 2, 2 * width), bf16),
        ),
        in_specs=[ANY] * 4,
        out_specs=(ANY,) * 4,
        scratch_shapes=[dma((30,)), dma((4,)), dma, dma((2,)), dma((2, 4))],
        compiler_params=pltpu.CompilerParams(
            has_side_effects=True, collective_id=1, vmem_limit_bytes=2**20
        ),
        name="scatter_heads",
    )(*(pltpu.with_memory_space_constraint(x, pltpu.HBM) for x in (queries, keys, values, hidden)))

    steps = tokens // 2 // rows
    tile = PAIR * rows
    o, kept = pl.pallas_call(
        attention_kernel,
        out_shape=(
            jax.ShapeDtypeStruct((tokens // 2, HS), bf16),
            jax.ShapeDtypeStruct(output_weight.shape, bf16),
        ),
        in_specs=[SMEM, VMEM, VMEM, VMEM, ANY],
        out_specs=(VMEM, ANY),
        scratch_shapes=[
            pltpu.VMEM((pl.cdiv(tokens, BK), tile, BK), f32),
            pltpu.VMEM((tile, HS), f32),
            pltpu.VMEM((tile, 2 * HS), f32),
            dma,
        ],
        compiler_params=pltpu.CompilerParams(vmem_limit_bytes=24 * 2**20),
        name="attend",
    )(request_length, qbuf, kbuf, vbuf, pltpu.with_memory_space_constraint(output_weight, pltpu.HBM))

    half = rows // 2
    chunks = 2 * width // COLS
    parts = len(PARTS)
    return pl.pallas_call(
        project_kernel,
        out_shape=jax.ShapeDtypeStruct((rows, 2 * width), bf16),
        in_specs=[SMEM, SMEM, ANY] + [VMEM] * 5,
        out_specs=ANY,
        scratch_shapes=[
            pltpu.VMEM((2, half, width), bf16),
            pltpu.VMEM((half, width), bf16),
            pltpu.VMEM((half, rank), f32),
            pltpu.VMEM((half, rank), f32),
            pltpu.VMEM((half, 2 * width), f32),
            pltpu.VMEM((chunks, half, COLS), bf16),
            pltpu.VMEM((chunks, half, COLS), bf16),
            pltpu.VMEM((half, rank), bf16),
            pltpu.VMEM((half, rank), bf16),
            pltpu.VMEM((half, 2 * width), bf16),
            dma((parts, 2, steps)), dma((parts,)),
            dma((parts, chunks, 2)), dma((parts, 2)), dma((parts, chunks, 3)),
        ],
        compiler_params=pltpu.CompilerParams(
            has_side_effects=True, collective_id=2, vmem_limit_bytes=16 * 2**20
        ),
        name="project",
    )(request_length, request_adapters, o, hidden, hbuf, kept, down, up)


def solution(mesh):
    return jax.shard_map(
        local,
        mesh=mesh,
        in_specs=(
            P("cfg", "seq", "head"),
            P("cfg", "seq", "head"),
            P("cfg", "seq", "head"),
            P("cfg", "seq", "head"),
            P("head", None),
            P(None, "head", None),
            P(None, None, "head"),
            P(),
            P(),
        ),
        out_specs=P("seq", "head"),
        check_vma=False,
    )
```

```python
import functools
import math

import jax
import jax.numpy as jnp
from jax import lax
from jax.experimental import pallas as pl
from jax.experimental.pallas import tpu as pltpu
from jax.sharding import PartitionSpec as P

MESH = pl.DeviceIdType.MESH
HS = 128
GUIDE = 5.0
BK = 2304
PAIR = 2
PARTS = ((0, 32), (32, 80))
COLS = 512
ANY = pl.BlockSpec(memory_space=pl.ANY)
SMEM = pl.BlockSpec(memory_space=pltpu.SMEM)
VMEM = pl.BlockSpec(memory_space=pltpu.VMEM)


def place(head, branch):
    y = head // 2
    x = 2 * (head % 2) + (y + branch) % 2
    p = jnp.where(head < 8, y * 4 + x, jnp.where(head == 8, 1 - branch, 11 - branch))
    return (p // 4) * 8 + branch * 4 + p % 4


def role(s):
    x, y, branch = s % 4, s // 8, (s // 4) % 2
    p = y * 4 + x
    board = (x + y) % 2 == branch
    late = jnp.where(p == 1 - branch, 8, 9)
    active = jnp.logical_or(board, jnp.logical_or(p == 1 - branch, p == 11 - branch))
    return active, jnp.where(board, y * 2 + x // 2, late), branch


def signal(semaphore, *device):
    pl.semaphore_signal(semaphore, inc=1, device_id=device, device_id_type=MESH)


def scatter_kernel(
    q_ref, k_ref, v_ref, hid_ref, kbuf, vbuf, qbuf, hbuf,
    send_sem, kv_sem, q_sem, hid_sem, fwd_sem,
):
    b = lax.axis_index("cfg")
    s = lax.axis_index("seq")
    g = lax.axis_index("head")
    rows = q_ref.shape[1]
    heads = q_ref.shape[2] // HS
    half = hbuf.shape[0]
    active, _, branch = role(s)
    seqs = 32

    barrier = pltpu.get_barrier_semaphore()
    signal(barrier, 1 - b, s, g)

    @pl.when(active)
    def _():
        @pl.loop(0, seqs)
        def _(i):
            t = (s + i) % seqs

            @pl.when(jnp.logical_not(jnp.logical_and(t == s, branch == b)))
            def _():
                signal(barrier, branch, t, g)

    own = jnp.where(jnp.logical_and(active, branch == b), 1, 0)
    pl.semaphore_wait(barrier, 2 * heads + 1 - own)

    groups = kv_sem.shape[0]
    per = kbuf.shape[0] // groups

    other = pltpu.make_async_remote_copy(
        src_ref=hid_ref.at[0, pl.ds(pl.multiple_of((1 - b) * half, 16), half), :],
        dst_ref=hbuf,
        send_sem=hid_sem.at[0],
        recv_sem=hid_sem.at[1],
        device_id=(1 - b, s, g),
        device_id_type=MESH,
    )

    row0 = pl.multiple_of(s * rows, 32)
    qrow0 = pl.multiple_of((s // 2) * rows, 32)
    kind = (
        (k_ref, lambda: kbuf.at[pl.ds(row0, rows), :], kv_sem.at[s // (32 // groups)], 0),
        (v_ref, lambda: vbuf.at[pl.ds(row0, rows), :], kv_sem.at[s // (32 // groups)], 1),
        (q_ref, lambda: qbuf.at[pl.ds(qrow0, rows), :], q_sem, s % 2),
    )

    def each(i, act, kinds=(0, 1, 2)):
        h = (i + s) % heads
        target = place(h, b)
        for n in kinds:
            src, dst, sem, core = kind[n]
            piece = src.at[0, :, pl.ds(pl.multiple_of(h * HS, HS), HS)]
            mine = jnp.logical_and(target == s, core == b)
            act(n, piece, dst(), sem, core, target, mine, i)

    def start(n, piece, dst, sem, core, target, mine, i):
        @pl.when(mine)
        def _():
            pltpu.make_async_copy(piece, dst, sem).start()

        @pl.when(jnp.logical_not(mine))
        def _():
            pltpu.make_async_remote_copy(
                src_ref=piece, dst_ref=dst, send_sem=send_sem.at[i * 3 + n], recv_sem=sem,
                device_id=(core, target, g), device_id_type=MESH,
            ).start()

    def finish(n, piece, dst, sem, core, target, mine, i):
        @pl.when(jnp.logical_not(mine))
        def _():
            pltpu.make_async_remote_copy(
                src_ref=piece, dst_ref=dst, send_sem=send_sem.at[i * 3 + n], recv_sem=sem,
                device_id=(core, target, g), device_id_type=MESH,
            ).wait_send()

    for n in range(3):

        @pl.loop(0, heads)
        def _(i):
            each(i, start, (n,))

    other.start()

    def forward(buf, n):
        part = buf.at[pl.ds(n * per, per), :]
        return pltpu.make_async_remote_copy(
            src_ref=part, dst_ref=part, send_sem=fwd_sem.at[0, n], recv_sem=fwd_sem.at[1, n],
            device_id=(1 - b, s, g), device_id_type=MESH,
        )

    def landed(buf, sem):
        pltpu.make_async_copy(buf, buf, sem).wait()

    for core, (got, came) in enumerate(((kbuf, vbuf), (vbuf, kbuf))):

        @pl.when(jnp.logical_and(active, b == core))
        def _():
            for n in range(groups):
                landed(got.at[pl.ds(n * per, per), :], kv_sem.at[n])
                forward(got, n).start()
            for n in range(groups):
                forward(got, n).wait_send()
                forward(came, n).wait_recv()
            landed(qbuf, q_sem)

    @pl.loop(0, heads)
    def _(i):
        each(i, finish)

    other.wait()


def attention_kernel(
    len_ref, q_ref, k_ref, v_ref, w_ref, o_ref, kept_ref, s_ref, m_ref, acc_ref, w_sem
):
    c = lax.axis_index("cfg")
    s = lax.axis_index("seq")
    active, _, _ = role(s)
    rows = acc_ref.shape[0]
    piece = rows // PAIR
    tokens = k_ref.shape[0]
    factor = math.log2(math.e) / math.sqrt(HS)
    fetch = pltpu.make_async_copy(w_ref, kept_ref, w_sem)
    fetch.start()
    e0 = len_ref[0]
    e1 = e0 + len_ref[1]
    e2 = e1 + len_ref[2]

    def segment(pos):
        return (
            (pos >= e0).astype(jnp.int32)
            + (pos >= e1).astype(jnp.int32)
            + (pos >= e2).astype(jnp.int32)
        )

    @pl.loop(0, jnp.where(active, q_ref.shape[0] // rows, 0))
    def _(tile):
        first = (2 * PAIR * tile + c) * piece
        last = first + (2 * PAIR - 1) * piece - 1
        own = pl.ds(pl.multiple_of(tile * rows, 32), rows)
        seg_first = segment(first)
        seg_last = segment(last)
        starts = (0, e0, e1, e2)
        ends = (e0, e1, e2, tokens)
        lo = jnp.int32(0)
        hi = jnp.int32(tokens)
        for n in range(4):
            lo = jnp.where(seg_first == n, starts[n], lo)
            hi = jnp.where(seg_last == n, ends[n], hi)
        base = (lo // 32) * 32
        rest = (hi - base) % BK
        large = (hi - base) // BK + jnp.where(rest > BK // 2, 1, 0)
        small = jnp.where(jnp.logical_and(rest > 0, rest <= BK // 2), 1, 0)
        single = seg_first == seg_last
        row = lax.broadcasted_iota(jnp.int32, (rows, 1), 0)
        seg_q = segment(first + row + (row // piece) * piece)
        m_ref[...] = jnp.full_like(m_ref, -1e30)

        def scores(n, size):
            logical = base + n * BK
            at = pl.multiple_of(jnp.minimum(logical, tokens - size), 32)
            whole = jnp.logical_and(
                single, jnp.logical_and(logical >= lo, logical + size <= hi)
            )

            def product():
                return lax.dot_general(
                    q_ref[own, :], k_ref[pl.ds(at, size), :], (((1,), (1,)), ((), ())),
                    preferred_element_type=jnp.float32,
                )

            def keep(score):
                s_ref[n, :, :size] = score
                widest = m_ref[...]
                for j in range(size // HS):
                    widest = jnp.maximum(widest, score[:, j * HS : (j + 1) * HS])
                m_ref[...] = widest

            @pl.when(whole)
            def _():
                keep(product())

            @pl.when(jnp.logical_not(whole))
            def _():
                pos = at + lax.broadcasted_iota(jnp.int32, (1, size), 1)
                seg_k = jnp.where(pos >= logical, segment(pos), -1)
                keep(jnp.where(seg_q == seg_k, product(), -jnp.inf))

        def weigh(n, size):
            at = pl.multiple_of(jnp.minimum(base + n * BK, tokens - size), 32)
            top = m_ref[...]
            weight = jnp.concatenate(
                [
                    jnp.exp2((s_ref[n, :, j * HS : (j + 1) * HS] - top) * factor).astype(
                        jnp.bfloat16
                    )
                    for j in range(size // HS)
                ],
                axis=1,
            )
            values = jnp.concatenate(
                [v_ref[pl.ds(at, size), :], jnp.ones((size, HS), jnp.bfloat16)], axis=1
            )
            acc_ref[...] += jnp.dot(weight, values, preferred_element_type=jnp.float32)

        def over_blocks(work):
            @pl.loop(0, large)
            def _(n):
                work(n, BK)

            @pl.loop(large, large + small)
            def _(n):
                work(n, BK // 2)

        over_blocks(scores)
        m_ref[...] = jnp.broadcast_to(
            jnp.max(m_ref[...], axis=1, keepdims=True), m_ref.shape
        )
        acc_ref[...] = jnp.zeros_like(acc_ref)
        over_blocks(weigh)
        o_ref[own, :] = (acc_ref[:, :HS] / acc_ref[:, HS:]).astype(o_ref.dtype)

    fetch.wait()


def project_kernel(
    len_ref, ad_ref, o_ref, hid_ref, hbuf, w_ref, down_ref, up_ref, out_ref,
    att, dv, inner, picked, pm, psend, precv, isend, irecv, outv,
    o_send, o_sem, p_sem, i_sem, out_sem,
):
    b = lax.axis_index("cfg")
    s = lax.axis_index("seq")
    g = lax.axis_index("head")
    active, head, branch = role(s)
    half, width = outv.shape
    rows = 2 * half
    heads = att.shape[2] // HS
    blocks = o_ref.shape[0] // rows
    chunks = range(width // COLS)
    top = pl.multiple_of(b * half, 16)

    barrier = pltpu.get_barrier_semaphore()
    signal(barrier, 1 - b, s, g)
    signal(barrier, b, s, 1 - g)

    for origin in range(2):

        @pl.loop(0, heads)
        def _(i):
            t = place((i + s) % heads, origin)

            @pl.when(jnp.logical_not(jnp.logical_and(t == s, s % 2 == b)))
            def _():
                signal(barrier, s % 2, t, g)

    own = jnp.where(s % 2 == b, 1, 0)
    pl.semaphore_wait(barrier, 2 + jnp.where(active, 2 * blocks - own, 0))

    def send_o(i, n, core, go):
        j = 2 * i + b
        first, count = PARTS[n]
        piece = o_ref.at[pl.ds(pl.multiple_of(i * rows + core * half + first, 16), count), :]
        dst = att.at[branch, pl.ds(first, count), pl.ds(pl.multiple_of(head * HS, HS), HS)]
        here = jnp.logical_and(j == s, core == b)

        @pl.when(here)
        def _():
            if go:
                pltpu.make_async_copy(piece, dst, o_sem.at[n]).start()

        @pl.when(jnp.logical_not(here))
        def _():
            copy = pltpu.make_async_remote_copy(
                src_ref=piece, dst_ref=dst, send_sem=o_send.at[n, core, i], recv_sem=o_sem.at[n],
                device_id=(core, j, g), device_id_type=MESH,
            )
            if go:
                copy.start()
            else:
                copy.wait_send()

    @pl.when(active)
    def _():
        for n in range(len(PARTS)):

            @pl.loop(0, blocks)
            def _(i):
                for core in range(2):
                    send_o((i + s // 2) % blocks, n, core, True)

    def partner(src, dst, sems):
        return pltpu.make_async_remote_copy(
            src_ref=src, dst_ref=dst, send_sem=sems.at[0], recv_sem=sems.at[1],
            device_id=(b, s, 1 - g), device_id_type=MESH,
        )

    rank = down_ref.shape[0] // 8
    pos = s * rows + b * half + lax.broadcasted_iota(jnp.int32, picked.shape, 0)
    lane = lax.broadcasted_iota(jnp.int32, picked.shape, 1)
    e0 = len_ref[0]
    e1 = e0 + len_ref[1]
    e2 = e1 + len_ref[2]
    adapter = jnp.where(
        pos < e1,
        jnp.where(pos < e0, ad_ref[0], ad_ref[1]),
        jnp.where(pos < e2, ad_ref[2], ad_ref[3]),
    )
    picked[...] = ((lane // rank) == adapter).astype(jnp.float32)
    scale_m = jnp.where(b == 0, GUIDE, 1.0 - GUIDE).astype(jnp.float32)
    scale_o = jnp.where(b == 0, 1.0 - GUIDE, GUIDE).astype(jnp.float32)
    hm = hid_ref[0, pl.ds(top, half), :].astype(jnp.float32)
    pm[...] = scale_m * hm + scale_o * hbuf[...].astype(jnp.float32)

    def column(c):
        return slice(c * COLS, (c + 1) * COLS)

    def weight(side, c):
        return w_ref[:, pl.ds(pl.multiple_of(side * width + c * COLS, COLS), COLS)]

    for n, (first, count) in enumerate(PARTS):
        sl = slice(first, first + count)
        came = att.at[:, pl.ds(first, count), :]
        pltpu.make_async_copy(came, came, o_sem.at[n]).wait()
        dv[sl, :] = (
            GUIDE * att[0, sl, :].astype(jnp.float32)
            + (1.0 - GUIDE) * att[1, sl, :].astype(jnp.float32)
        ).astype(jnp.bfloat16)
        for c in chunks:
            psend[c, sl, :] = jnp.dot(
                dv[sl, :], weight(1 - g, c), preferred_element_type=jnp.float32
            ).astype(jnp.bfloat16)
            partner(psend.at[c, sl, :], precv.at[c, sl, :], p_sem.at[n, c]).start()
            if c == 0:
                inner[sl, :] = (
                    lax.dot_general(
                        dv[sl, :], down_ref[...], (((1,), (1,)), ((), ())),
                        preferred_element_type=jnp.float32,
                    )
                    * picked[sl, :]
                )
                isend[sl, :] = inner[sl, :].astype(jnp.bfloat16)
                partner(isend.at[sl, :], irecv.at[sl, :], i_sem.at[n]).start()
    for c in chunks:
        pm[:, column(c)] += jnp.dot(
            dv[...], weight(g, c), preferred_element_type=jnp.float32
        )
    for n, (first, count) in enumerate(PARTS):
        sl = slice(first, first + count)
        partner(isend.at[sl, :], irecv.at[sl, :], i_sem.at[n]).wait()
    both = (inner[...] + irecv[...].astype(jnp.float32)).astype(jnp.bfloat16)
    for c in chunks:
        pm[:, column(c)] += jnp.dot(both, up_ref[:, column(c)], preferred_element_type=jnp.float32)
    last = []
    for n, (first, count) in enumerate(PARTS):
        sl = slice(first, first + count)
        for c in chunks:
            partner(psend.at[c, sl, :], precv.at[c, sl, :], p_sem.at[n, c]).wait()
            outv[sl, column(c)] = (
                pm[sl, column(c)] + precv[c, sl, :].astype(jnp.float32)
            ).astype(jnp.bfloat16)
            piece = outv.at[sl, pl.ds(c * COLS, COLS)]
            result = out_ref.at[pl.ds(pl.multiple_of(top + first, 16), count), pl.ds(c * COLS, COLS)]
            last.append(
                pltpu.make_async_remote_copy(
                    src_ref=piece, dst_ref=result,
                    send_sem=out_sem.at[n, c, 0], recv_sem=out_sem.at[n, c, 1],
                    device_id=(1 - b, s, g), device_id_type=MESH,
                )
            )
            last.append(pltpu.make_async_copy(piece, result, out_sem.at[n, c, 2]))
            last[-2].start()
            last[-1].start()

    @pl.when(active)
    def _():
        for n in range(len(PARTS)):

            @pl.loop(0, blocks)
            def _(i):
                for core in range(2):
                    send_o(i, n, core, False)

    for copy in last:
        copy.wait()


def local(
    hidden, queries, keys, values, output_weight, adapter_down_weight, adapter_up_weight,
    request_adapters, request_length,
):
    rows, width = queries.shape[1:]
    tokens = rows * 32
    bf16, f32 = jnp.bfloat16, jnp.float32
    dma = pltpu.SemaphoreType.DMA
    down = adapter_down_weight.transpose(0, 2, 1).reshape(-1, width)
    up = adapter_up_weight.reshape(-1, adapter_up_weight.shape[2])
    rank = up.shape[0]

    kbuf, vbuf, qbuf, hbuf = pl.pallas_call(
        scatter_kernel,
        out_shape=(
            jax.ShapeDtypeStruct((tokens, HS), bf16),
            jax.ShapeDtypeStruct((tokens, HS), bf16),
            jax.ShapeDtypeStruct((tokens // 2, HS), bf16),
            jax.ShapeDtypeStruct((rows // 2, 2 * width), bf16),
        ),
        in_specs=[ANY] * 4,
        out_specs=(ANY,) * 4,
        scratch_shapes=[dma((30,)), dma((4,)), dma, dma((2,)), dma((2, 4))],
        compiler_params=pltpu.CompilerParams(
            has_side_effects=True, collective_id=1, vmem_limit_bytes=2**20
        ),
        name="scatter_heads",
    )(*(pltpu.with_memory_space_constraint(x, pltpu.HBM) for x in (queries, keys, values, hidden)))

    steps = tokens // 2 // rows
    tile = PAIR * rows
    o, kept = pl.pallas_call(
        attention_kernel,
        out_shape=(
            jax.ShapeDtypeStruct((tokens // 2, HS), bf16),
            jax.ShapeDtypeStruct(output_weight.shape, bf16),
        ),
        in_specs=[SMEM, VMEM, VMEM, VMEM, ANY],
        out_specs=(VMEM, ANY),
        scratch_shapes=[
            pltpu.VMEM((pl.cdiv(tokens, BK), tile, BK), f32),
            pltpu.VMEM((tile, HS), f32),
            pltpu.VMEM((tile, 2 * HS), f32),
            dma,
        ],
        compiler_params=pltpu.CompilerParams(vmem_limit_bytes=24 * 2**20),
        name="attend",
    )(request_length, qbuf, kbuf, vbuf, pltpu.with_memory_space_constraint(output_weight, pltpu.HBM))

    half = rows // 2
    chunks = 2 * width // COLS
    parts = len(PARTS)
    return pl.pallas_call(
        project_kernel,
        out_shape=jax.ShapeDtypeStruct((rows, 2 * width), bf16),
        in_specs=[SMEM, SMEM, ANY] + [VMEM] * 5,
        out_specs=ANY,
        scratch_shapes=[
            pltpu.VMEM((2, half, width), bf16),
            pltpu.VMEM((half, width), bf16),
            pltpu.VMEM((half, rank), f32),
            pltpu.VMEM((half, rank), f32),
            pltpu.VMEM((half, 2 * width), f32),
            pltpu.VMEM((chunks, half, COLS), bf16),
            pltpu.VMEM((chunks, half, COLS), bf16),
            pltpu.VMEM((half, rank), bf16),
            pltpu.VMEM((half, rank), bf16),
            pltpu.VMEM((half, 2 * width), bf16),
            dma((parts, 2, steps)), dma((parts,)),
            dma((parts, chunks, 2)), dma((parts, 2)), dma((parts, chunks, 3)),
        ],
        compiler_params=pltpu.CompilerParams(
            has_side_effects=True, collective_id=2, vmem_limit_bytes=16 * 2**20
        ),
        name="project",
    )(request_length, request_adapters, o, hidden, hbuf, kept, down, up)


def solution(mesh):
    return jax.shard_map(
        local,
        mesh=mesh,
        in_specs=(
            P("cfg", "seq", "head"),
            P("cfg", "seq", "head"),
            P("cfg", "seq", "head"),
            P("cfg", "seq", "head"),
            P("head", None),
            P(None, "head", None),
            P(None, None, "head"),
            P(),
            P(),
        ),
        out_specs=P("seq", "head"),
        check_vma=False,
    )
```

```python
import functools
import math

import jax
import jax.numpy as jnp
from jax import lax
from jax.experimental import pallas as pl
from jax.experimental.pallas import tpu as pltpu
from jax.sharding import PartitionSpec as P

MESH = pl.DeviceIdType.MESH
HS = 128
GUIDE = 5.0
BK = 2304
PAIR = 2
PARTS = ((0, 32), (32, 80))
COLS = 512
ANY = pl.BlockSpec(memory_space=pl.ANY)
SMEM = pl.BlockSpec(memory_space=pltpu.SMEM)
VMEM = pl.BlockSpec(memory_space=pltpu.VMEM)


def place(head, branch):
    y = head // 2
    x = 2 * (head % 2) + (y + branch) % 2
    p = jnp.where(head < 8, y * 4 + x, jnp.where(head == 8, 1 - branch, 11 - branch))
    return (p // 4) * 8 + branch * 4 + p % 4


def role(s):
    x, y, branch = s % 4, s // 8, (s // 4) % 2
    p = y * 4 + x
    board = (x + y) % 2 == branch
    late = jnp.where(p == 1 - branch, 8, 9)
    active = jnp.logical_or(board, jnp.logical_or(p == 1 - branch, p == 11 - branch))
    return active, jnp.where(board, y * 2 + x // 2, late), branch


def signal(semaphore, *device):
    pl.semaphore_signal(semaphore, inc=1, device_id=device, device_id_type=MESH)


def scatter_kernel(
    q_ref, k_ref, v_ref, hid_ref, kbuf, vbuf, qbuf, hbuf,
    send_sem, kv_sem, q_sem, hid_sem, fwd_sem,
):
    b = lax.axis_index("cfg")
    s = lax.axis_index("seq")
    g = lax.axis_index("head")
    rows = q_ref.shape[1]
    heads = q_ref.shape[2] // HS
    half = hbuf.shape[0]
    active, _, branch = role(s)
    seqs = 32

    barrier = pltpu.get_barrier_semaphore()
    signal(barrier, 1 - b, s, g)

    @pl.when(active)
    def _():
        @pl.loop(0, seqs)
        def _(i):
            t = (s + i) % seqs

            @pl.when(jnp.logical_not(jnp.logical_and(t == s, branch == b)))
            def _():
                signal(barrier, branch, t, g)

    own = jnp.where(jnp.logical_and(active, branch == b), 1, 0)
    pl.semaphore_wait(barrier, 2 * heads + 1 - own)

    groups = kv_sem.shape[0]
    per = kbuf.shape[0] // groups

    other = pltpu.make_async_remote_copy(
        src_ref=hid_ref.at[0, pl.ds(pl.multiple_of((1 - b) * half, 16), half), :],
        dst_ref=hbuf,
        send_sem=hid_sem.at[0],
        recv_sem=hid_sem.at[1],
        device_id=(1 - b, s, g),
        device_id_type=MESH,
    )

    row0 = pl.multiple_of(s * rows, 32)
    qrow0 = pl.multiple_of((s // 2) * rows, 32)
    kind = (
        (k_ref, lambda: kbuf.at[pl.ds(row0, rows), :], kv_sem.at[s // (32 // groups)], 0),
        (v_ref, lambda: vbuf.at[pl.ds(row0, rows), :], kv_sem.at[s // (32 // groups)], 1),
        (q_ref, lambda: qbuf.at[pl.ds(qrow0, rows), :], q_sem, s % 2),
    )

    def each(i, act, kinds=(0, 1, 2)):
        h = (i + s) % heads
        target = place(h, b)
        for n in kinds:
            src, dst, sem, core = kind[n]
            piece = src.at[0, :, pl.ds(pl.multiple_of(h * HS, HS), HS)]
            mine = jnp.logical_and(target == s, core == b)
            act(n, piece, dst(), sem, core, target, mine, i)

    def start(n, piece, dst, sem, core, target, mine, i):
        @pl.when(mine)
        def _():
            pltpu.make_async_copy(piece, dst, sem).start()

        @pl.when(jnp.logical_not(mine))
        def _():
            pltpu.make_async_remote_copy(
                src_ref=piece, dst_ref=dst, send_sem=send_sem.at[i * 3 + n], recv_sem=sem,
                device_id=(core, target, g), device_id_type=MESH,
            ).start()

    def finish(n, piece, dst, sem, core, target, mine, i):
        @pl.when(jnp.logical_not(mine))
        def _():
            pltpu.make_async_remote_copy(
                src_ref=piece, dst_ref=dst, send_sem=send_sem.at[i * 3 + n], recv_sem=sem,
                device_id=(core, target, g), device_id_type=MESH,
            ).wait_send()

    for n in range(3):

        @pl.loop(0, heads)
        def _(i):
            each(i, start, (n,))

    other.start()

    def forward(buf, n):
        part = buf.at[pl.ds(n * per, per), :]
        return pltpu.make_async_remote_copy(
            src_ref=part, dst_ref=part, send_sem=fwd_sem.at[0, n], recv_sem=fwd_sem.at[1, n],
            device_id=(1 - b, s, g), device_id_type=MESH,
        )

    def landed(buf, sem):
        pltpu.make_async_copy(buf, buf, sem).wait()

    for core, (got, came) in enumerate(((kbuf, vbuf), (vbuf, kbuf))):

        @pl.when(jnp.logical_and(active, b == core))
        def _():
            for n in range(groups):
                landed(got.at[pl.ds(n * per, per), :], kv_sem.at[n])
                forward(got, n).start()
            for n in range(groups):
                forward(got, n).wait_send()
                forward(came, n).wait_recv()
            landed(qbuf, q_sem)

    @pl.loop(0, heads)
    def _(i):
        each(i, finish)

    other.wait()


def attention_kernel(
    len_ref, q_ref, k_ref, v_ref, w_ref, o_ref, kept_ref, s_ref, m_ref, acc_ref, w_sem
):
    c = lax.axis_index("cfg")
    s = lax.axis_index("seq")
    active, _, _ = role(s)
    rows = acc_ref.shape[0]
    piece = rows // PAIR
    tokens = k_ref.shape[0]
    factor = math.log2(math.e) / math.sqrt(HS)
    fetch = pltpu.make_async_copy(w_ref, kept_ref, w_sem)
    fetch.start()
    e0 = len_ref[0]
    e1 = e0 + len_ref[1]
    e2 = e1 + len_ref[2]

    def segment(pos):
        return (
            (pos >= e0).astype(jnp.int32)
            + (pos >= e1).astype(jnp.int32)
            + (pos >= e2).astype(jnp.int32)
        )

    @pl.loop(0, jnp.where(active, q_ref.shape[0] // rows, 0))
    def _(tile):
        first = (2 * PAIR * tile + c) * piece
        last = first + (2 * PAIR - 1) * piece - 1
        own = pl.ds(pl.multiple_of(tile * rows, 32), rows)
        seg_first = segment(first)
        seg_last = segment(last)
        starts = (0, e0, e1, e2)
        ends = (e0, e1, e2, tokens)
        lo = jnp.int32(0)
        hi = jnp.int32(tokens)
        for n in range(4):
            lo = jnp.where(seg_first == n, starts[n], lo)
            hi = jnp.where(seg_last == n, ends[n], hi)
        base = (lo // 32) * 32
        rest = (hi - base) % BK
        large = (hi - base) // BK + jnp.where(rest > BK // 2, 1, 0)
        small = jnp.where(jnp.logical_and(rest > 0, rest <= BK // 2), 1, 0)
        single = seg_first == seg_last
        row = lax.broadcasted_iota(jnp.int32, (rows, 1), 0)
        seg_q = segment(first + row + (row // piece) * piece)
        m_ref[...] = jnp.full_like(m_ref, -1e30)

        def scores(n, size):
            logical = base + n * BK
            at = pl.multiple_of(jnp.minimum(logical, tokens - size), 32)
            whole = jnp.logical_and(
                single, jnp.logical_and(logical >= lo, logical + size <= hi)
            )

            def product():
                return lax.dot_general(
                    q_ref[own, :], k_ref[pl.ds(at, size), :], (((1,), (1,)), ((), ())),
                    preferred_element_type=jnp.float32,
                )

            def keep(score):
                s_ref[n, :, :size] = score
                widest = m_ref[...]
                for j in range(size // HS):
                    widest = jnp.maximum(widest, score[:, j * HS : (j + 1) * HS])
                m_ref[...] = widest

            @pl.when(whole)
            def _():
                keep(product())

            @pl.when(jnp.logical_not(whole))
            def _():
                pos = at + lax.broadcasted_iota(jnp.int32, (1, size), 1)
                seg_k = jnp.where(pos >= logical, segment(pos), -1)
                keep(jnp.where(seg_q == seg_k, product(), -jnp.inf))

        def weigh(n, size):
            at = pl.multiple_of(jnp.minimum(base + n * BK, tokens - size), 32)
            top = m_ref[...]
            weight = jnp.concatenate(
                [
                    jnp.exp2((s_ref[n, :, j * HS : (j + 1) * HS] - top) * factor).astype(
                        jnp.bfloat16
                    )
                    for j in range(size // HS)
                ],
                axis=1,
            )
            values = jnp.concatenate(
                [v_ref[pl.ds(at, size), :], jnp.ones((size, HS), jnp.bfloat16)], axis=1
            )
            acc_ref[...] += jnp.dot(weight, values, preferred_element_type=jnp.float32)

        def over_blocks(work):
            @pl.loop(0, large)
            def _(n):
                work(n, BK)

            @pl.loop(large, large + small)
            def _(n):
                work(n, BK // 2)

        over_blocks(scores)
        m_ref[...] = jnp.broadcast_to(
            jnp.max(m_ref[...], axis=1, keepdims=True), m_ref.shape
        )
        acc_ref[...] = jnp.zeros_like(acc_ref)
        over_blocks(weigh)
        o_ref[own, :] = (acc_ref[:, :HS] / acc_ref[:, HS:]).astype(o_ref.dtype)

    fetch.wait()


def project_kernel(
    len_ref, ad_ref, o_ref, hid_ref, hbuf, w_ref, down_ref, up_ref, out_ref,
    att, dv, inner, picked, pm, psend, precv, isend, irecv, outv,
    o_send, o_sem, p_sem, i_sem, out_sem,
):
    b = lax.axis_index("cfg")
    s = lax.axis_index("seq")
    g = lax.axis_index("head")
    active, head, branch = role(s)
    half, width = outv.shape
    rows = 2 * half
    heads = att.shape[2] // HS
    blocks = o_ref.shape[0] // rows
    chunks = range(width // COLS)
    top = pl.multiple_of(b * half, 16)

    barrier = pltpu.get_barrier_semaphore()
    signal(barrier, 1 - b, s, g)
    signal(barrier, b, s, 1 - g)

    for origin in range(2):

        @pl.loop(0, heads)
        def _(i):
            t = place((i + s) % heads, origin)

            @pl.when(jnp.logical_not(jnp.logical_and(t == s, s % 2 == b)))
            def _():
                signal(barrier, s % 2, t, g)

    own = jnp.where(s % 2 == b, 1, 0)
    pl.semaphore_wait(barrier, 2 + jnp.where(active, 2 * blocks - own, 0))

    def send_o(i, n, core, go):
        j = 2 * i + b
        first, count = PARTS[n]
        piece = o_ref.at[pl.ds(pl.multiple_of(i * rows + core * half + first, 16), count), :]
        dst = att.at[branch, pl.ds(first, count), pl.ds(pl.multiple_of(head * HS, HS), HS)]
        here = jnp.logical_and(j == s, core == b)

        @pl.when(here)
        def _():
            if go:
                pltpu.make_async_copy(piece, dst, o_sem.at[n]).start()

        @pl.when(jnp.logical_not(here))
        def _():
            copy = pltpu.make_async_remote_copy(
                src_ref=piece, dst_ref=dst, send_sem=o_send.at[n, core, i], recv_sem=o_sem.at[n],
                device_id=(core, j, g), device_id_type=MESH,
            )
            if go:
                copy.start()
            else:
                copy.wait_send()

    @pl.when(active)
    def _():
        for n in range(len(PARTS)):

            @pl.loop(0, blocks)
            def _(i):
                for core in range(2):
                    send_o(i, n, core, True)

    def partner(src, dst, sems):
        return pltpu.make_async_remote_copy(
            src_ref=src, dst_ref=dst, send_sem=sems.at[0], recv_sem=sems.at[1],
            device_id=(b, s, 1 - g), device_id_type=MESH,
        )

    rank = down_ref.shape[0] // 8
    pos = s * rows + b * half + lax.broadcasted_iota(jnp.int32, picked.shape, 0)
    lane = lax.broadcasted_iota(jnp.int32, picked.shape, 1)
    e0 = len_ref[0]
    e1 = e0 + len_ref[1]
    e2 = e1 + len_ref[2]
    adapter = jnp.where(
        pos < e1,
        jnp.where(pos < e0, ad_ref[0], ad_ref[1]),
        jnp.where(pos < e2, ad_ref[2], ad_ref[3]),
    )
    picked[...] = ((lane // rank) == adapter).astype(jnp.float32)
    scale_m = jnp.where(b == 0, GUIDE, 1.0 - GUIDE).astype(jnp.float32)
    scale_o = jnp.where(b == 0, 1.0 - GUIDE, GUIDE).astype(jnp.float32)
    hm = hid_ref[0, pl.ds(top, half), :].astype(jnp.float32)
    pm[...] = scale_m * hm + scale_o * hbuf[...].astype(jnp.float32)

    def column(c):
        return slice(c * COLS, (c + 1) * COLS)

    def weight(side, c):
        return w_ref[:, pl.ds(pl.multiple_of(side * width + c * COLS, COLS), COLS)]

    for n, (first, count) in enumerate(PARTS):
        sl = slice(first, first + count)
        came = att.at[:, pl.ds(first, count), :]
        pltpu.make_async_copy(came, came, o_sem.at[n]).wait()
        dv[sl, :] = (
            GUIDE * att[0, sl, :].astype(jnp.float32)
            + (1.0 - GUIDE) * att[1, sl, :].astype(jnp.float32)
        ).astype(jnp.bfloat16)
        for c in chunks:
            psend[c, sl, :] = jnp.dot(
                dv[sl, :], weight(1 - g, c), preferred_element_type=jnp.float32
            ).astype(jnp.bfloat16)
            partner(psend.at[c, sl, :], precv.at[c, sl, :], p_sem.at[n, c]).start()
            if c == 0:
                inner[sl, :] = (
                    lax.dot_general(
                        dv[sl, :], down_ref[...], (((1,), (1,)), ((), ())),
                        preferred_element_type=jnp.float32,
                    )
                    * picked[sl, :]
                )
                isend[sl, :] = inner[sl, :].astype(jnp.bfloat16)
                partner(isend.at[sl, :], irecv.at[sl, :], i_sem.at[n]).start()
    for c in chunks:
        pm[:, column(c)] += jnp.dot(
            dv[...], weight(g, c), preferred_element_type=jnp.float32
        )
    for n, (first, count) in enumerate(PARTS):
        sl = slice(first, first + count)
        partner(isend.at[sl, :], irecv.at[sl, :], i_sem.at[n]).wait()
    both = (inner[...] + irecv[...].astype(jnp.float32)).astype(jnp.bfloat16)
    for c in chunks:
        pm[:, column(c)] += jnp.dot(both, up_ref[:, column(c)], preferred_element_type=jnp.float32)
    last = []
    for n, (first, count) in enumerate(PARTS):
        sl = slice(first, first + count)
        for c in chunks:
            partner(psend.at[c, sl, :], precv.at[c, sl, :], p_sem.at[n, c]).wait()
            outv[sl, column(c)] = (
                pm[sl, column(c)] + precv[c, sl, :].astype(jnp.float32)
            ).astype(jnp.bfloat16)
            piece = outv.at[sl, pl.ds(c * COLS, COLS)]
            result = out_ref.at[pl.ds(pl.multiple_of(top + first, 16), count), pl.ds(c * COLS, COLS)]
            last.append(
                pltpu.make_async_remote_copy(
                    src_ref=piece, dst_ref=result,
                    send_sem=out_sem.at[n, c, 0], recv_sem=out_sem.at[n, c, 1],
                    device_id=(1 - b, s, g), device_id_type=MESH,
                )
            )
            last.append(pltpu.make_async_copy(piece, result, out_sem.at[n, c, 2]))
            last[-2].start()
            last[-1].start()

    @pl.when(active)
    def _():
        for n in range(len(PARTS)):

            @pl.loop(0, blocks)
            def _(i):
                for core in range(2):
                    send_o(i, n, core, False)

    for copy in last:
        copy.wait()


def local(
    hidden, queries, keys, values, output_weight, adapter_down_weight, adapter_up_weight,
    request_adapters, request_length,
):
    rows, width = queries.shape[1:]
    tokens = rows * 32
    bf16, f32 = jnp.bfloat16, jnp.float32
    dma = pltpu.SemaphoreType.DMA
    down = adapter_down_weight.transpose(0, 2, 1).reshape(-1, width)
    up = adapter_up_weight.reshape(-1, adapter_up_weight.shape[2])
    rank = up.shape[0]

    kbuf, vbuf, qbuf, hbuf = pl.pallas_call(
        scatter_kernel,
        out_shape=(
            jax.ShapeDtypeStruct((tokens, HS), bf16),
            jax.ShapeDtypeStruct((tokens, HS), bf16),
            jax.ShapeDtypeStruct((tokens // 2, HS), bf16),
            jax.ShapeDtypeStruct((rows // 2, 2 * width), bf16),
        ),
        in_specs=[ANY] * 4,
        out_specs=(ANY,) * 4,
        scratch_shapes=[dma((30,)), dma((4,)), dma, dma((2,)), dma((2, 4))],
        compiler_params=pltpu.CompilerParams(
            has_side_effects=True, collective_id=1, vmem_limit_bytes=2**20
        ),
        name="scatter_heads",
    )(*(pltpu.with_memory_space_constraint(x, pltpu.HBM) for x in (queries, keys, values, hidden)))

    steps = tokens // 2 // rows
    tile = PAIR * rows
    o, kept = pl.pallas_call(
        attention_kernel,
        out_shape=(
            jax.ShapeDtypeStruct((tokens // 2, HS), bf16),
            jax.ShapeDtypeStruct(output_weight.shape, bf16),
        ),
        in_specs=[SMEM, VMEM, VMEM, VMEM, ANY],
        out_specs=(VMEM, ANY),
        scratch_shapes=[
            pltpu.VMEM((pl.cdiv(tokens, BK), tile, BK), f32),
            pltpu.VMEM((tile, HS), f32),
            pltpu.VMEM((tile, 2 * HS), f32),
            dma,
        ],
        compiler_params=pltpu.CompilerParams(vmem_limit_bytes=24 * 2**20),
        name="attend",
    )(request_length, qbuf, kbuf, vbuf, pltpu.with_memory_space_constraint(output_weight, pltpu.HBM))

    half = rows // 2
    chunks = 2 * width // COLS
    parts = len(PARTS)
    return pl.pallas_call(
        project_kernel,
        out_shape=jax.ShapeDtypeStruct((rows, 2 * width), bf16),
        in_specs=[SMEM, SMEM, ANY] + [VMEM] * 5,
        out_specs=ANY,
        scratch_shapes=[
            pltpu.VMEM((2, half, width), bf16),
            pltpu.VMEM((half, width), bf16),
            pltpu.VMEM((half, rank), f32),
            pltpu.VMEM((half, rank), f32),
            pltpu.VMEM((half, 2 * width), f32),
            pltpu.VMEM((chunks, half, COLS), bf16),
            pltpu.VMEM((chunks, half, COLS), bf16),
            pltpu.VMEM((half, rank), bf16),
            pltpu.VMEM((half, rank), bf16),
            pltpu.VMEM((half, 2 * width), bf16),
            dma((parts, 2, steps)), dma((parts,)),
            dma((parts, chunks, 2)), dma((parts, 2)), dma((parts, chunks, 3)),
        ],
        compiler_params=pltpu.CompilerParams(
            has_side_effects=True, collective_id=2, vmem_limit_bytes=16 * 2**20
        ),
        name="project",
    )(request_length, request_adapters, o, hidden, hbuf, kept, down, up)


def solution(mesh):
    return jax.shard_map(
        local,
        mesh=mesh,
        in_specs=(
            P("cfg", "seq", "head"),
            P("cfg", "seq", "head"),
            P("cfg", "seq", "head"),
            P("cfg", "seq", "head"),
            P("head", None),
            P(None, "head", None),
            P(None, None, "head"),
            P(),
            P(),
        ),
        out_specs=P("seq", "head"),
        check_vma=False,
    )
```

```python
import functools
import math

import jax
import jax.numpy as jnp
from jax import lax
from jax.experimental import pallas as pl
from jax.experimental.pallas import tpu as pltpu
from jax.sharding import PartitionSpec as P

MESH = pl.DeviceIdType.MESH
HS = 128
GUIDE = 5.0
BK = 2304
PAIR = 2
PARTS = ((0, 32), (32, 80))
COLS = 512
ANY = pl.BlockSpec(memory_space=pl.ANY)
SMEM = pl.BlockSpec(memory_space=pltpu.SMEM)
VMEM = pl.BlockSpec(memory_space=pltpu.VMEM)


def place(head, branch):
    y = head // 2
    x = 2 * (head % 2) + (y + branch) % 2
    p = jnp.where(head < 8, y * 4 + x, jnp.where(head == 8, 1 - branch, 11 - branch))
    return (p // 4) * 8 + branch * 4 + p % 4


def role(s):
    x, y, branch = s % 4, s // 8, (s // 4) % 2
    p = y * 4 + x
    board = (x + y) % 2 == branch
    late = jnp.where(p == 1 - branch, 8, 9)
    active = jnp.logical_or(board, jnp.logical_or(p == 1 - branch, p == 11 - branch))
    return active, jnp.where(board, y * 2 + x // 2, late), branch


def signal(semaphore, *device):
    pl.semaphore_signal(semaphore, inc=1, device_id=device, device_id_type=MESH)


def scatter_kernel(
    q_ref, k_ref, v_ref, hid_ref, kbuf, vbuf, qbuf, hbuf,
    send_sem, kv_sem, q_sem, hid_sem, fwd_sem,
):
    b = lax.axis_index("cfg")
    s = lax.axis_index("seq")
    g = lax.axis_index("head")
    rows = q_ref.shape[1]
    heads = q_ref.shape[2] // HS
    half = hbuf.shape[0]
    active, _, branch = role(s)
    seqs = 32

    barrier = pltpu.get_barrier_semaphore()
    signal(barrier, 1 - b, s, g)

    @pl.when(active)
    def _():
        @pl.loop(0, seqs)
        def _(i):
            t = (s + i) % seqs

            @pl.when(jnp.logical_not(jnp.logical_and(t == s, branch == b)))
            def _():
                signal(barrier, branch, t, g)

    own = jnp.where(jnp.logical_and(active, branch == b), 1, 0)
    pl.semaphore_wait(barrier, 2 * heads + 1 - own)

    groups = kv_sem.shape[0]
    per = kbuf.shape[0] // groups

    other = pltpu.make_async_remote_copy(
        src_ref=hid_ref.at[0, pl.ds(pl.multiple_of((1 - b) * half, 16), half), :],
        dst_ref=hbuf,
        send_sem=hid_sem.at[0],
        recv_sem=hid_sem.at[1],
        device_id=(1 - b, s, g),
        device_id_type=MESH,
    )

    row0 = pl.multiple_of(s * rows, 32)
    qrow0 = pl.multiple_of((s // 2) * rows, 32)
    kind = (
        (k_ref, lambda: kbuf.at[pl.ds(row0, rows), :], kv_sem.at[s // (32 // groups)], 0),
        (v_ref, lambda: vbuf.at[pl.ds(row0, rows), :], kv_sem.at[s // (32 // groups)], 1),
        (q_ref, lambda: qbuf.at[pl.ds(qrow0, rows), :], q_sem, s % 2),
    )

    def each(i, act, kinds=(0, 1, 2)):
        h = (i + s) % heads
        target = place(h, b)
        for n in kinds:
            src, dst, sem, core = kind[n]
            piece = src.at[0, :, pl.ds(pl.multiple_of(h * HS, HS), HS)]
            mine = jnp.logical_and(target == s, core == b)
            act(n, piece, dst(), sem, core, target, mine, i)

    def start(n, piece, dst, sem, core, target, mine, i):
        @pl.when(mine)
        def _():
            pltpu.make_async_copy(piece, dst, sem).start()

        @pl.when(jnp.logical_not(mine))
        def _():
            pltpu.make_async_remote_copy(
                src_ref=piece, dst_ref=dst, send_sem=send_sem.at[i * 3 + n], recv_sem=sem,
                device_id=(core, target, g), device_id_type=MESH,
            ).start()

    def finish(n, piece, dst, sem, core, target, mine, i):
        @pl.when(jnp.logical_not(mine))
        def _():
            pltpu.make_async_remote_copy(
                src_ref=piece, dst_ref=dst, send_sem=send_sem.at[i * 3 + n], recv_sem=sem,
                device_id=(core, target, g), device_id_type=MESH,
            ).wait_send()

    for n in range(3):

        @pl.loop(0, heads)
        def _(i):
            each(i, start, (n,))

    other.start()

    def forward(buf, n):
        part = buf.at[pl.ds(n * per, per), :]
        return pltpu.make_async_remote_copy(
            src_ref=part, dst_ref=part, send_sem=fwd_sem.at[0, n], recv_sem=fwd_sem.at[1, n],
            device_id=(1 - b, s, g), device_id_type=MESH,
        )

    def landed(buf, sem):
        pltpu.make_async_copy(buf, buf, sem).wait()

    for core, (got, came) in enumerate(((kbuf, vbuf), (vbuf, kbuf))):

        @pl.when(jnp.logical_and(active, b == core))
        def _():
            for n in range(groups):
                landed(got.at[pl.ds(n * per, per), :], kv_sem.at[n])
                forward(got, n).start()
            for n in range(groups):
                forward(got, n).wait_send()
                forward(came, n).wait_recv()
            landed(qbuf, q_sem)

    @pl.loop(0, heads)
    def _(i):
        each(i, finish)

    other.wait()


def attention_kernel(
    len_ref, q_ref, k_ref, v_ref, w_ref, o_ref, kept_ref, s_ref, m_ref, acc_ref, w_sem
):
    c = lax.axis_index("cfg")
    s = lax.axis_index("seq")
    active, _, _ = role(s)
    rows = acc_ref.shape[0]
    piece = rows // PAIR
    tokens = k_ref.shape[0]
    factor = math.log2(math.e) / math.sqrt(HS)
    fetch = pltpu.make_async_copy(w_ref, kept_ref, w_sem)
    fetch.start()
    e0 = len_ref[0]
    e1 = e0 + len_ref[1]
    e2 = e1 + len_ref[2]

    def segment(pos):
        return (
            (pos >= e0).astype(jnp.int32)
            + (pos >= e1).astype(jnp.int32)
            + (pos >= e2).astype(jnp.int32)
        )

    @pl.loop(0, jnp.where(active, q_ref.shape[0] // rows, 0))
    def _(tile):
        first = (2 * PAIR * tile + c) * piece
        last = first + (2 * PAIR - 1) * piece - 1
        own = pl.ds(pl.multiple_of(tile * rows, 32), rows)
        seg_first = segment(first)
        seg_last = segment(last)
        starts = (0, e0, e1, e2)
        ends = (e0, e1, e2, tokens)
        lo = jnp.int32(0)
        hi = jnp.int32(tokens)
        for n in range(4):
            lo = jnp.where(seg_first == n, starts[n], lo)
            hi = jnp.where(seg_last == n, ends[n], hi)
        base = (lo // 32) * 32
        rest = (hi - base) % BK
        large = (hi - base) // BK + jnp.where(rest > BK // 2, 1, 0)
        small = jnp.where(jnp.logical_and(rest > 0, rest <= BK // 2), 1, 0)
        single = seg_first == seg_last
        row = lax.broadcasted_iota(jnp.int32, (rows, 1), 0)
        seg_q = segment(first + row + (row // piece) * piece)
        m_ref[...] = jnp.full_like(m_ref, -1e30)

        def scores(n, size):
            logical = base + n * BK
            at = pl.multiple_of(jnp.minimum(logical, tokens - size), 32)
            whole = jnp.logical_and(
                single, jnp.logical_and(logical >= lo, logical + size <= hi)
            )

            def product():
                return lax.dot_general(
                    q_ref[own, :], k_ref[pl.ds(at, size), :], (((1,), (1,)), ((), ())),
                    preferred_element_type=jnp.float32,
                )

            def keep(score):
                s_ref[n, :, :size] = score
                widest = m_ref[...]
                for j in range(size // HS):
                    widest = jnp.maximum(widest, score[:, j * HS : (j + 1) * HS])
                m_ref[...] = widest

            @pl.when(whole)
            def _():
                keep(product())

            @pl.when(jnp.logical_not(whole))
            def _():
                pos = at + lax.broadcasted_iota(jnp.int32, (1, size), 1)
                seg_k = jnp.where(pos >= logical, segment(pos), -1)
                keep(jnp.where(seg_q == seg_k, product(), -jnp.inf))

        def weigh(n, size):
            at = pl.multiple_of(jnp.minimum(base + n * BK, tokens - size), 32)
            top = m_ref[...]
            weight = jnp.concatenate(
                [
                    jnp.exp2((s_ref[n, :, j * HS : (j + 1) * HS] - top) * factor).astype(
                        jnp.bfloat16
                    )
                    for j in range(size // HS)
                ],
                axis=1,
            )
            values = jnp.concatenate(
                [v_ref[pl.ds(at, size), :], jnp.ones((size, HS), jnp.bfloat16)], axis=1
            )
            acc_ref[...] += jnp.dot(weight, values, preferred_element_type=jnp.float32)

        def over_blocks(work):
            @pl.loop(0, large)
            def _(n):
                work(n, BK)

            @pl.loop(large, large + small)
            def _(n):
                work(n, BK // 2)

        over_blocks(scores)
        m_ref[...] = jnp.broadcast_to(
            jnp.max(m_ref[...], axis=1, keepdims=True), m_ref.shape
        )
        acc_ref[...] = jnp.zeros_like(acc_ref)
        over_blocks(weigh)
        o_ref[own, :] = (acc_ref[:, :HS] / acc_ref[:, HS:]).astype(o_ref.dtype)

    fetch.wait()


def project_kernel(
    len_ref, ad_ref, o_ref, hid_ref, hbuf, w_ref, down_ref, up_ref, out_ref,
    att, dv, inner, picked, pm, psend, precv, isend, irecv, outv,
    o_send, o_sem, p_sem, i_sem, out_sem,
):
    b = lax.axis_index("cfg")
    s = lax.axis_index("seq")
    g = lax.axis_index("head")
    active, head, branch = role(s)
    half, width = outv.shape
    rows = 2 * half
    heads = att.shape[2] // HS
    blocks = o_ref.shape[0] // rows
    chunks = range(width // COLS)
    top = pl.multiple_of(b * half, 16)

    barrier = pltpu.get_barrier_semaphore()
    signal(barrier, 1 - b, s, g)
    signal(barrier, b, s, 1 - g)

    for origin in range(2):

        @pl.loop(0, heads)
        def _(i):
            t = place((i + s) % heads, origin)

            @pl.when(jnp.logical_not(jnp.logical_and(t == s, s % 2 == b)))
            def _():
                signal(barrier, s % 2, t, g)

    own = jnp.where(s % 2 == b, 1, 0)
    pl.semaphore_wait(barrier, 2 + jnp.where(active, 2 * blocks - own, 0))

    def send_o(i, n, core, go):
        j = 2 * i + b
        first, count = PARTS[n]
        piece = o_ref.at[pl.ds(pl.multiple_of(i * rows + core * half + first, 16), count), :]
        dst = att.at[branch, pl.ds(first, count), pl.ds(pl.multiple_of(head * HS, HS), HS)]
        here = jnp.logical_and(j == s, core == b)

        @pl.when(here)
        def _():
            if go:
                pltpu.make_async_copy(piece, dst, o_sem.at[n]).start()

        @pl.when(jnp.logical_not(here))
        def _():
            copy = pltpu.make_async_remote_copy(
                src_ref=piece, dst_ref=dst, send_sem=o_send.at[n, core, i], recv_sem=o_sem.at[n],
                device_id=(core, j, g), device_id_type=MESH,
            )
            if go:
                copy.start()
            else:
                copy.wait_send()

    @pl.when(active)
    def _():
        for n in range(len(PARTS)):

            @pl.loop(0, blocks)
            def _(i):
                for core in range(2):
                    send_o(i, n, core, True)

    def partner(src, dst, sems):
        return pltpu.make_async_remote_copy(
            src_ref=src, dst_ref=dst, send_sem=sems.at[0], recv_sem=sems.at[1],
            device_id=(b, s, 1 - g), device_id_type=MESH,
        )

    rank = down_ref.shape[0] // 8
    pos = s * rows + b * half + lax.broadcasted_iota(jnp.int32, picked.shape, 0)
    lane = lax.broadcasted_iota(jnp.int32, picked.shape, 1)
    e0 = len_ref[0]
    e1 = e0 + len_ref[1]
    e2 = e1 + len_ref[2]
    adapter = jnp.where(
        pos < e1,
        jnp.where(pos < e0, ad_ref[0], ad_ref[1]),
        jnp.where(pos < e2, ad_ref[2], ad_ref[3]),
    )
    picked[...] = ((lane // rank) == adapter).astype(jnp.float32)
    scale_m = jnp.where(b == 0, GUIDE, 1.0 - GUIDE).astype(jnp.float32)
    scale_o = jnp.where(b == 0, 1.0 - GUIDE, GUIDE).astype(jnp.float32)
    hm = hid_ref[0, pl.ds(top, half), :].astype(jnp.float32)
    pm[...] = scale_m * hm + scale_o * hbuf[...].astype(jnp.float32)

    def column(c):
        return slice(c * COLS, (c + 1) * COLS)

    def weight(side, c):
        return w_ref[:, pl.ds(pl.multiple_of(side * width + c * COLS, COLS), COLS)]

    for n, (first, count) in enumerate(PARTS):
        sl = slice(first, first + count)
        came = att.at[:, pl.ds(first, count), :]
        pltpu.make_async_copy(came, came, o_sem.at[n]).wait()
        dv[sl, :] = (
            GUIDE * att[0, sl, :].astype(jnp.float32)
            + (1.0 - GUIDE) * att[1, sl, :].astype(jnp.float32)
        ).astype(jnp.bfloat16)
        for c in chunks:
            psend[c, sl, :] = jnp.dot(
                dv[sl, :], weight(1 - g, c), preferred_element_type=jnp.float32
            ).astype(jnp.bfloat16)
            partner(psend.at[c, sl, :], precv.at[c, sl, :], p_sem.at[n, c]).start()
            if c == 0:
                inner[sl, :] = (
                    lax.dot_general(
                        dv[sl, :], down_ref[...], (((1,), (1,)), ((), ())),
                        preferred_element_type=jnp.float32,
                    )
                    * picked[sl, :]
                )
                isend[sl, :] = inner[sl, :].astype(jnp.bfloat16)
                partner(isend.at[sl, :], irecv.at[sl, :], i_sem.at[n]).start()
    for n, (first, count) in enumerate(PARTS):
        sl = slice(first, first + count)
        partner(isend.at[sl, :], irecv.at[sl, :], i_sem.at[n]).wait()
    both = (inner[...] + irecv[...].astype(jnp.float32)).astype(jnp.bfloat16)
    for c in chunks:
        pm[:, column(c)] += jnp.dot(
            dv[...], weight(g, c), preferred_element_type=jnp.float32
        ) + jnp.dot(both, up_ref[:, column(c)], preferred_element_type=jnp.float32)
    last = []
    for n, (first, count) in enumerate(PARTS):
        sl = slice(first, first + count)
        for c in chunks:
            partner(psend.at[c, sl, :], precv.at[c, sl, :], p_sem.at[n, c]).wait()
            outv[sl, column(c)] = (
                pm[sl, column(c)] + precv[c, sl, :].astype(jnp.float32)
            ).astype(jnp.bfloat16)
            piece = outv.at[sl, pl.ds(c * COLS, COLS)]
            result = out_ref.at[pl.ds(pl.multiple_of(top + first, 16), count), pl.ds(c * COLS, COLS)]
            last.append(
                pltpu.make_async_remote_copy(
                    src_ref=piece, dst_ref=result,
                    send_sem=out_sem.at[n, c, 0], recv_sem=out_sem.at[n, c, 1],
                    device_id=(1 - b, s, g), device_id_type=MESH,
                )
            )
            last.append(pltpu.make_async_copy(piece, result, out_sem.at[n, c, 2]))
            last[-2].start()
            last[-1].start()

    @pl.when(active)
    def _():
        for n in range(len(PARTS)):

            @pl.loop(0, blocks)
            def _(i):
                for core in range(2):
                    send_o(i, n, core, False)

    for copy in last:
        copy.wait()


def local(
    hidden, queries, keys, values, output_weight, adapter_down_weight, adapter_up_weight,
    request_adapters, request_length,
):
    rows, width = queries.shape[1:]
    tokens = rows * 32
    bf16, f32 = jnp.bfloat16, jnp.float32
    dma = pltpu.SemaphoreType.DMA
    down = adapter_down_weight.transpose(0, 2, 1).reshape(-1, width)
    up = adapter_up_weight.reshape(-1, adapter_up_weight.shape[2])
    rank = up.shape[0]

    kbuf, vbuf, qbuf, hbuf = pl.pallas_call(
        scatter_kernel,
        out_shape=(
            jax.ShapeDtypeStruct((tokens, HS), bf16),
            jax.ShapeDtypeStruct((tokens, HS), bf16),
            jax.ShapeDtypeStruct((tokens // 2, HS), bf16),
            jax.ShapeDtypeStruct((rows // 2, 2 * width), bf16),
        ),
        in_specs=[ANY] * 4,
        out_specs=(ANY,) * 4,
        scratch_shapes=[dma((30,)), dma((4,)), dma, dma((2,)), dma((2, 4))],
        compiler_params=pltpu.CompilerParams(
            has_side_effects=True, collective_id=1, vmem_limit_bytes=2**20
        ),
        name="scatter_heads",
    )(*(pltpu.with_memory_space_constraint(x, pltpu.HBM) for x in (queries, keys, values, hidden)))

    steps = tokens // 2 // rows
    tile = PAIR * rows
    o, kept = pl.pallas_call(
        attention_kernel,
        out_shape=(
            jax.ShapeDtypeStruct((tokens // 2, HS), bf16),
            jax.ShapeDtypeStruct(output_weight.shape, bf16),
        ),
        in_specs=[SMEM, VMEM, VMEM, VMEM, ANY],
        out_specs=(VMEM, ANY),
        scratch_shapes=[
            pltpu.VMEM((pl.cdiv(tokens, BK), tile, BK), f32),
            pltpu.VMEM((tile, HS), f32),
            pltpu.VMEM((tile, 2 * HS), f32),
            dma,
        ],
        compiler_params=pltpu.CompilerParams(vmem_limit_bytes=24 * 2**20),
        name="attend",
    )(request_length, qbuf, kbuf, vbuf, pltpu.with_memory_space_constraint(output_weight, pltpu.HBM))

    half = rows // 2
    chunks = 2 * width // COLS
    parts = len(PARTS)
    return pl.pallas_call(
        project_kernel,
        out_shape=jax.ShapeDtypeStruct((rows, 2 * width), bf16),
        in_specs=[SMEM, SMEM, ANY] + [VMEM] * 5,
        out_specs=ANY,
        scratch_shapes=[
            pltpu.VMEM((2, half, width), bf16),
            pltpu.VMEM((half, width), bf16),
            pltpu.VMEM((half, rank), f32),
            pltpu.VMEM((half, rank), f32),
            pltpu.VMEM((half, 2 * width), f32),
            pltpu.VMEM((chunks, half, COLS), bf16),
            pltpu.VMEM((chunks, half, COLS), bf16),
            pltpu.VMEM((half, rank), bf16),
            pltpu.VMEM((half, rank), bf16),
            pltpu.VMEM((half, 2 * width), bf16),
            dma((parts, 2, steps)), dma((parts,)),
            dma((parts, chunks, 2)), dma((parts, 2)), dma((parts, chunks, 3)),
        ],
        compiler_params=pltpu.CompilerParams(
            has_side_effects=True, collective_id=2, vmem_limit_bytes=16 * 2**20
        ),
        name="project",
    )(request_length, request_adapters, o, hidden, hbuf, kept, down, up)


def solution(mesh):
    return jax.shard_map(
        local,
        mesh=mesh,
        in_specs=(
            P("cfg", "seq", "head"),
            P("cfg", "seq", "head"),
            P("cfg", "seq", "head"),
            P("cfg", "seq", "head"),
            P("head", None),
            P(None, "head", None),
            P(None, None, "head"),
            P(),
            P(),
        ),
        out_specs=P("seq", "head"),
        check_vma=False,
    )
```
